256 devices in a mesh: atom: 16 (over x, z_hi, core), refl: 16 (over z_lo, y).
Axes of the slice: x: 4, y: 4, z: 8 (z_hi: 2, z_lo: 4; z = z_hi * 4 + z_lo), core: 2. Of those that a mesh axis runs over, the one named last changes fastest.
Arguments:
- positions: float32 [3, 524288], P(None, ('atom', 'refl')), may hold values from 0 to 1
- occupancy: float32 [524288], P(('atom', 'refl')), may hold values from 0.3 to 1
- bfactor: float32 [524288], P(('atom', 'refl')), may hold values from 1 to 8
- atom_type: int32 [524288], P(('atom', 'refl')), may hold values from 0 to 7
- miller: int32 [3, 2048], P(None, 'refl'), may hold values from -48 to 48
- observed: float32 [2048], P('refl'), may hold values from 0.2 to 5
- weight: float32 [2048], P('refl'), may hold values from 0.3 to 3
- coef_a: float32 [8, 4], replicated, may hold values from 0.3 to 3
- coef_b: float32 [8, 4], replicated, may hold values from 0.5 to 20
- coef_c: float32 [8], replicated, may hold values from 0.1 to 1
Outputs:
- gradient: float32 [3, 524288], P(None, ('atom', 'refl'))
- residual: float32 [2048], P('refl')
The draws below stay inside these ranges and needn't reach their ends.
All inputs are finite; a program needn't handle non-finite values.
Results may differ from the reference program's by a relative error of at most 0.0003.
Values sent between devices are 32-bit elements; how exact they have to be, the bound alone decides.
A program may use at most 64 MiB of HBM per device.

```python
import math
import jax
import jax.numpy as jnp
from jax import lax

TYPES = 8
GAUSS = 4
ATOMS = 524288
REFL = 2048


def touch_ends(array, own_key, low, top_value):
    place = [jax.random.randint(jax.random.fold_in(own_key, axis), (), 0, length) for axis, length in enumerate(array.shape)]
    widest = array.shape.index(max(array.shape))
    neighbour = place[:widest] + [(place[widest] + 1) % array.shape[widest]] + place[widest + 1:]
    return array.at[tuple(place)].set(low).at[tuple(neighbour)].set(top_value)


def level_of(rng, extent, split, least, largest):
    level = 1.0
    for axis_at, shards_of in split:
        draws = jax.random.uniform(jax.random.fold_in(jax.random.fold_in(rng, 6), axis_at), (shards_of,), jnp.float32, least / len(split), largest / len(split))
        level = level * jnp.repeat(jnp.exp(draws), extent[axis_at] // shards_of).reshape((-1,) + (1,) * (len(extent) - 1 - axis_at))
    return level


def setup_inputs(seed: int = 0) -> dict:
    keys = jax.random.split(jax.random.key(seed), 11)
    positions = jnp.clip(1.0 * jax.random.uniform(keys[0], (3, ATOMS), jnp.float32) ** level_of(keys[0], (3, ATOMS), ((1, 256),), -0.2, 0.2), 0.0, 1.0)
    occupancy = jnp.clip(jnp.exp(math.log(1.0) - 1.2039728 * jax.random.uniform(keys[1], (ATOMS,), jnp.float32) ** level_of(keys[1], (ATOMS,), ((0, 256),), -0.2, 0.2)), 0.3, 1.0)
    bfactor = jnp.clip(jnp.exp(math.log(8.0) - 2.0794415 * jax.random.uniform(keys[2], (ATOMS,), jnp.float32) ** level_of(keys[2], (ATOMS,), ((0, 256),), -0.2, 0.2)), 1.0, 8.0)
    atom_type = touch_ends(jax.random.randint(keys[3], (ATOMS,), 0, TYPES), jax.random.fold_in(keys[3], 1), 0, TYPES - 1).astype(jnp.int32)
    miller = touch_ends(jax.random.randint(keys[4], (3, REFL), -48, 49), jax.random.fold_in(keys[4], 1), -48, 48).astype(jnp.int32)
    observed = jnp.clip(jnp.exp(math.log(5.0) - 3.218876 * jax.random.uniform(keys[5], (REFL,), jnp.float32) ** level_of(keys[5], (REFL,), ((0, 16),), -0.2, 0.2)), 0.2, 5.0)
    weight = jnp.clip(jnp.exp(math.log(3.0) - 2.3025851 * jax.random.uniform(keys[6], (REFL,), jnp.float32) ** level_of(keys[6], (REFL,), ((0, 16),), -0.2, 0.2)), 0.3, 3.0)
    coef_a = jnp.clip(jnp.exp(jax.random.uniform(keys[7], (TYPES, GAUSS), jnp.float32, math.log(0.3), math.log(3.0))), 0.3, 3.0)
    coef_b = jnp.clip(jnp.exp(jax.random.uniform(keys[8], (TYPES, GAUSS), jnp.float32, math.log(0.5), math.log(20.0))), 0.5, 20.0)
    coef_c = jnp.clip(jax.random.uniform(keys[9], (TYPES,), jnp.float32, 0.1, 1.0), 0.1, 1.0)
    return dict(positions=positions, occupancy=occupancy, bfactor=bfactor, atom_type=atom_type, miller=miller, observed=observed, weight=weight, coef_a=coef_a, coef_b=coef_b, coef_c=coef_c)


two_pi = 6.283185307179586
cell_edge = 100.0

def form_table(coef_a, coef_b, coef_c, s2):
    return lax.optimization_barrier(jnp.sum(coef_a[:, :, None] * jnp.exp(-0.25 * coef_b[:, :, None] * s2[None, None, :]), axis=1)) + coef_c[:, None]

def block_terms(stack, hklf, s2, table):
    turns = stack[0][:, None] * hklf[0][None] + stack[1][:, None] * hklf[1][None] + stack[2][:, None] * hklf[2][None]
    phase = two_pi * turns
    kinds = (stack[5][:, None] == jnp.arange(table.shape[0], dtype=stack.dtype)[None]).astype(stack.dtype)
    form = jnp.dot(kinds, table, precision=lax.Precision.HIGHEST)
    weighted = stack[3][:, None] * jnp.exp(-0.25 * stack[4][:, None] * s2[None]) * form
    return (weighted, jnp.cos(phase), jnp.sin(phase))

def reference(positions, occupancy, bfactor, atom_type, miller, observed, weight, coef_a, coef_b, coef_c):
    stack = jnp.concatenate([positions, occupancy[None], bfactor[None], atom_type.astype(positions.dtype)[None]], axis=0)
    hklf = miller.astype(positions.dtype)
    s2 = lax.optimization_barrier(jnp.sum(hklf * hklf, axis=0)) / (cell_edge * cell_edge)
    table = form_table(coef_a, coef_b, coef_c, s2)
    width = math.gcd(ATOMS, 4096)
    blocks = stack.reshape(6, ATOMS // width, width).transpose(1, 0, 2)

    def forward(block):
        weighted, cosv, sinv = block_terms(block, hklf, s2, table)
        return jnp.stack([lax.optimization_barrier(jnp.sum(weighted * cosv, axis=0)), lax.optimization_barrier(jnp.sum(weighted * sinv, axis=0))])
    sums = lax.optimization_barrier(jnp.sum(lax.map(forward, blocks), axis=0)) / math.sqrt(ATOMS)
    real_part, imag_part = (sums[0], sums[1])
    amp = jnp.sqrt(real_part * real_part + imag_part * imag_part + 0.25)
    scale = jnp.sum(weight * observed * amp) / jnp.sum(weight * amp * amp)
    residual = scale * amp - observed
    coeff = 2.0 * weight * scale * residual / (amp * math.sqrt(REFL))
    along_b = coeff * imag_part
    along_a = coeff * real_part

    def backward(block):
        weighted, cosv, sinv = block_terms(block, hklf, s2, table)
        inner = weighted * (along_b[None] * cosv - along_a[None] * sinv)
        return jnp.einsum('dr,nr->dn', hklf, inner, precision=lax.Precision.HIGHEST)
    terms = lax.map(backward, blocks).transpose(1, 0, 2).reshape(3, ATOMS)
    gradient = terms * (two_pi / math.sqrt(ATOMS))
    return (gradient, residual)
```

```python
import functools
import math

import jax
import jax.numpy as jnp
from jax import lax
from jax.experimental import pallas as pl
from jax.experimental.pallas import tpu as pltpu
from jax.sharding import PartitionSpec as P

MESH = pl.DeviceIdType.MESH
two_pi = 6.283185307179586
cell_edge = 100.0
top = 48
TYPES, GAUSS = 8, 4
LANES = 128
unroll_f, unroll_b = 32, 32


def rotate(ac, as_, bc, bs):
    return ac * bc - as_ * bs, ac * bs + as_ * bc


def fold_rows(vregs):
    row = lax.broadcasted_iota(jnp.int32, (8, LANES), 0)
    for shift in (4, 2, 1):
        low = (row & shift) == 0
        half = len(vregs) // 2
        merged = []
        for n in range(half):
            a, b = vregs[n], vregs[n + half]
            keep = jnp.where(low, a, b)
            if shift == 4:
                move = pltpu.roll(jnp.where(low, b, a), 4, 0)
            else:
                move = jnp.where(low, pltpu.roll(a, 8 - shift, 0), pltpu.roll(b, shift, 0))
            merged.append(keep + move)
        vregs = merged
    return vregs[0]


def kernel(
    n_atom, n_refl,
    pos_ref, occ_ref, bf_ref, type_ref, miller_ref, obs_ref, weight_ref, ca_ref, cb_ref, cc_ref,
    grad_ref, resid_ref,
    tx, ty, tz, store, form_rows, form_t, rows, idx_v, hs, ks, ls, sums, part, reduced, mine, total_in, every,
    bu, bv, bh, bk, bl,
    g_send, g_recv, r_send, r_recv, a_send, a_recv, e_send, e_recv, i_sem,
):
    me_a = lax.axis_index("atom")
    me_r = lax.axis_index("refl")
    tiles = occ_ref.shape[0]
    refl = n_refl * LANES

    barrier = pltpu.get_barrier_semaphore()

    def greet(s, _):
        pl.semaphore_signal(barrier, inc=1, device_id=(me_a, lax.rem(me_r + s, n_refl)), device_id_type=MESH)
        return 0

    def greet_a(s, _):
        pl.semaphore_signal(barrier, inc=1, device_id=(lax.rem(me_a + s, n_atom), me_r), device_id_type=MESH)
        return 0

    lax.fori_loop(1, n_refl, greet, 0)
    lax.fori_loop(1, n_atom, greet_a, 0)

    rows[me_r] = miller_ref[...]

    pl.semaphore_wait(barrier, n_refl - 1 + n_atom - 1)

    def gather_copy(s):
        peer = lax.rem(me_r + s, n_refl)
        return pltpu.make_async_remote_copy(
            src_ref=rows.at[me_r], dst_ref=rows.at[me_r],
            send_sem=g_send.at[peer], recv_sem=g_recv.at[me_r],
            device_id=(me_a, peer), device_id_type=MESH,
        )

    def gather_wait(s):
        peer = lax.rem(me_r + s, n_refl)
        return pltpu.make_async_remote_copy(
            src_ref=rows.at[me_r], dst_ref=rows.at[peer],
            send_sem=g_send.at[peer], recv_sem=g_recv.at[peer],
            device_id=(me_a, peer), device_id_type=MESH,
        )

    def g_start(s, _):
        gather_copy(s).start()
        return 0

    lax.fori_loop(1, n_refl, g_start, 0)

    first = []
    for d in range(3):
        x = jnp.concatenate([pos_ref[d : d + 1, a * LANES : (a + 1) * LANES] for a in range(tiles)], axis=0)
        turn = two_pi * (x - jnp.round(x))
        first.append((jnp.cos(turn), jnp.sin(turn)))
    decay = bf_ref[...] * (-0.25 / (cell_edge * cell_edge))
    occ = occ_ref[...]

    def table_step(m, carry):
        mf = m.astype(jnp.float32)
        damp = jnp.exp(decay * (mf * mf))
        after = []
        for d, table in enumerate((tx, ty, tz)):
            c, s = carry[2 * d], carry[2 * d + 1]
            scale = damp * occ if d == 2 else damp
            table[top + m, 0] = c * scale
            table[top + m, 1] = s * scale
            table[top - m, 0] = c * scale
            table[top - m, 1] = -(s * scale)
            after += list(rotate(c, s, *first[d]))
        return tuple(after)

    one = jnp.ones((tiles, LANES), jnp.float32)
    zero = jnp.zeros((tiles, LANES), jnp.float32)
    lax.fori_loop(0, top + 1, table_step, (one, zero) * 3)

    def g_wait(s, _):
        gather_wait(s).wait_recv()
        return 0

    lax.fori_loop(1, n_refl, g_wait, 0)

    for d in range(3):
        for b in range(n_refl):
            idx_v[d, :, b * LANES : (b + 1) * LANES] = rows[b, d : d + 1, :] + top
    to_smem = [
        pltpu.make_async_copy(idx_v.at[d, 0], dst, i_sem.at[d]) for d, dst in enumerate((hs, ks, ls))
    ]
    for copy in to_smem:
        copy.start()

    hf, kf, lf = (rows[:, d, :].astype(jnp.float32) for d in range(3))
    s2 = (hf * hf + kf * kf + lf * lf) / (cell_edge * cell_edge)
    for t in range(TYPES):
        form = ca_ref[t, 0] * jnp.exp(-0.25 * cb_ref[t, 0] * s2)
        for g in range(1, GAUSS):
            form = form + ca_ref[t, g] * jnp.exp(-0.25 * cb_ref[t, g] * s2)
        form_t[:, t, :] = form + cc_ref[t]
    pad = jnp.zeros((LANES - TYPES, LANES), jnp.float32)
    for b in range(n_refl):
        form_rows[b * LANES : (b + 1) * LANES, :] = jnp.concatenate([form_t[b], pad], axis=0).T

    for copy in to_smem:
        copy.wait()

    kind = [type_ref[v * 8 : (v + 1) * 8, :] for v in range(tiles // 8)]

    def reduce_copy(b):
        return pltpu.make_async_remote_copy(
            src_ref=part.at[b], dst_ref=reduced.at[me_r],
            send_sem=r_send.at[b], recv_sem=r_recv.at[me_r],
            device_id=(me_a, b), device_id_type=MESH,
        )

    def reduce_wait(b):
        return pltpu.make_async_remote_copy(
            src_ref=part.at[b], dst_ref=reduced.at[b],
            send_sem=r_send.at[b], recv_sem=r_recv.at[b],
            device_id=(me_a, b), device_id_type=MESH,
        )

    def forward_block(step, _):
        b = lax.rem(me_r + 1 + step, n_refl)
        base = pl.multiple_of(b * LANES, LANES)

        def chunk(i, _):
            local0 = pl.multiple_of(i * unroll_f, unroll_f)
            r0 = base + local0
            parts = []
            for u in range(unroll_f):
                r = r0 + u
                h, k, l = hs[r], ks[r], ls[r]
                form_row = jnp.broadcast_to(form_rows[pl.ds(r, 1), :], (8, LANES))
                real, imag = None, None
                for v in range(tiles // 8):
                    off = v * 8
                    c, s = rotate(
                        tx[h, 0, off : off + 8, :], tx[h, 1, off : off + 8, :],
                        ty[k, 0, off : off + 8, :], ty[k, 1, off : off + 8, :],
                    )
                    c, s = rotate(c, s, tz[l, 0, off : off + 8, :], tz[l, 1, off : off + 8, :])
                    form = jnp.take_along_axis(form_row, kind[v], axis=1, mode="promise_in_bounds")
                    c = c * form
                    s = s * form
                    store[r, 0, off : off + 8, :] = c
                    store[r, 1, off : off + 8, :] = s
                    real = c if real is None else real + c
                    imag = s if imag is None else imag + s
                parts.append((real, imag))
            for g in range(unroll_f // 8):
                for j in range(2):
                    sums[j, pl.ds(local0 + g * 8, 8), :] = fold_rows([parts[g * 8 + u][j] for u in range(8)])
            return 0

        lax.fori_loop(0, LANES // unroll_f, chunk, 0)
        for j in range(2):
            part[b, j : j + 1, :] = jnp.sum(sums[j].T, axis=0, keepdims=True)

        @pl.when(step < n_refl - 1)
        def _():
            reduce_copy(b).start()

        return 0

    lax.fori_loop(0, n_refl, forward_block, 0)
    reduced[me_r] = part[me_r]

    def r_wait(s, _):
        reduce_wait(lax.rem(me_r + s, n_refl)).wait_recv()
        return 0

    lax.fori_loop(1, n_refl, r_wait, 0)
    mine[...] = jnp.sum(reduced[...], axis=0)
    total_in[me_a] = mine[...]

    def atom_copy(s, slot):
        peer = lax.rem(me_a + s, n_atom)
        return pltpu.make_async_remote_copy(
            src_ref=mine, dst_ref=total_in.at[me_a if slot is None else peer],
            send_sem=a_send.at[peer], recv_sem=a_recv.at[me_a if slot is None else peer],
            device_id=(peer, me_r), device_id_type=MESH,
        )

    def a_start(s, _):
        atom_copy(s, None).start()
        return 0

    def a_wait(s, _):
        atom_copy(s, 1).wait_recv()
        return 0

    lax.fori_loop(1, n_atom, a_start, 0)

    for b in range(n_refl):
        for d, wide in enumerate((bh, bk, bl)):
            wide[b * LANES : (b + 1) * LANES, :] = jnp.broadcast_to(rows[b, d : d + 1, :].astype(jnp.float32), (LANES, LANES)).T

    lax.fori_loop(1, n_atom, a_wait, 0)
    every[me_r, 0:2, :] = jnp.sum(total_in[...], axis=0)
    every[me_r, 2:3, :] = obs_ref[...]
    every[me_r, 3:4, :] = weight_ref[...]

    def every_copy(s, slot):
        peer = lax.rem(me_r + s, n_refl)
        return pltpu.make_async_remote_copy(
            src_ref=every.at[me_r], dst_ref=every.at[me_r if slot is None else peer],
            send_sem=e_send.at[peer], recv_sem=e_recv.at[me_r if slot is None else peer],
            device_id=(me_a, peer), device_id_type=MESH,
        )

    def e_start(s, _):
        every_copy(s, None).start()
        return 0

    def e_wait(s, _):
        every_copy(s, 1).wait_recv()
        return 0

    lax.fori_loop(1, n_refl, e_start, 0)
    lax.fori_loop(1, n_refl, e_wait, 0)

    atoms = tiles * LANES * n_atom * n_refl
    inv_atoms = 1.0 / math.sqrt(atoms)
    real_part = every[:, 0, :] * inv_atoms
    imag_part = every[:, 1, :] * inv_atoms
    amp = jnp.sqrt(real_part * real_part + imag_part * imag_part + 0.25)
    obs = every[:, 2, :]
    weight = every[:, 3, :]
    over = jnp.sum(weight * obs * amp, axis=(0, 1), keepdims=True)
    under = jnp.sum(weight * amp * amp, axis=(0, 1), keepdims=True)
    scale = over / under
    resid = scale * amp - obs
    coeff = 2.0 * weight * scale * resid / (amp * math.sqrt(refl)) * (two_pi * inv_atoms)
    along_b = coeff * imag_part
    along_a = coeff * real_part
    sums[0, 0:n_refl, :] = resid
    resid_ref[...] = sums[0, pl.ds(me_r, 1), :]
    for b in range(n_refl):
        bu[b * LANES : (b + 1) * LANES, :] = jnp.broadcast_to(along_b[b : b + 1, :], (LANES, LANES)).T
        bv[b * LANES : (b + 1) * LANES, :] = jnp.broadcast_to(along_a[b : b + 1, :], (LANES, LANES)).T

    def backward_chunk(i, acc):
        acc = [list(a) for a in acc]
        r0 = pl.multiple_of(i * unroll_b, unroll_b)
        for u in range(unroll_b):
            r = r0 + u
            wide = [jnp.broadcast_to(w[pl.ds(r, 1), :], (8, LANES)) for w in (bu, bv, bh, bk, bl)]
            for v in range(tiles // 8):
                off = v * 8
                inner = wide[0] * store[r, 0, off : off + 8, :] - wide[1] * store[r, 1, off : off + 8, :]
                for d in range(3):
                    acc[d][v] = acc[d][v] + wide[2 + d] * inner
        return tuple(tuple(a) for a in acc)

    none = jnp.zeros((8, LANES), jnp.float32)
    acc = lax.fori_loop(0, refl // unroll_b, backward_chunk, ((none,) * (tiles // 8),) * 3)
    for d in range(3):
        for v in range(tiles // 8):
            for a in range(8):
                t = v * 8 + a
                grad_ref[d : d + 1, t * LANES : (t + 1) * LANES] = acc[d][v][a : a + 1, :]

    def finish(s, _):
        gather_wait(s).wait_send()
        reduce_wait(lax.rem(me_r + s, n_refl)).wait_send()
        every_copy(s, 1).wait_send()
        return 0

    def finish_a(s, _):
        atom_copy(s, 1).wait_send()
        return 0

    lax.fori_loop(1, n_refl, finish, 0)
    lax.fori_loop(1, n_atom, finish_a, 0)


def solution(mesh):
    n_atom, n_refl = mesh.shape["atom"], mesh.shape["refl"]

    def local(positions, occupancy, bfactor, atom_type, miller, observed, weight, coef_a, coef_b, coef_c):
        shard = positions.shape[1]
        tiles = shard // LANES
        refl = miller.shape[1] * n_refl
        vmem = pl.BlockSpec(memory_space=pltpu.VMEM)
        smem = pl.BlockSpec(memory_space=pltpu.SMEM)
        f32 = jnp.float32
        table = pltpu.VMEM((2 * top + 1, 2, tiles, LANES), f32)
        wide = pltpu.VMEM((refl, LANES), f32)
        pair_r = pltpu.VMEM((n_refl, 2, LANES), f32)
        dma_r = pltpu.SemaphoreType.DMA((n_refl,))
        dma_a = pltpu.SemaphoreType.DMA((n_atom,))
        gradient, residual = pl.pallas_call(
            functools.partial(kernel, n_atom, n_refl),
            out_shape=(
                jax.ShapeDtypeStruct((3, shard), f32),
                jax.ShapeDtypeStruct((1, LANES), f32),
            ),
            in_specs=[vmem] * 7 + [smem] * 3,
            out_specs=(vmem, vmem),
            scratch_shapes=[
                table, table, table,
                pltpu.VMEM((refl, 2, tiles, LANES), f32),
                wide,
                pltpu.VMEM((n_refl, TYPES, LANES), f32),
                pltpu.VMEM((n_refl, 3, LANES), jnp.int32),
                pltpu.VMEM((3, 1, refl), jnp.int32),
                pltpu.SMEM((refl,), jnp.int32),
                pltpu.SMEM((refl,), jnp.int32),
                pltpu.SMEM((refl,), jnp.int32),
                pltpu.VMEM((2, LANES, LANES), f32),
                pair_r, pair_r,
                pltpu.VMEM((2, LANES), f32),
                pltpu.VMEM((n_atom, 2, LANES), f32),
                pltpu.VMEM((n_refl, 4, LANES), f32),
                wide, wide, wide, wide, wide,
                dma_r, dma_r, dma_r, dma_r, dma_a, dma_a, dma_r, dma_r,
                pltpu.SemaphoreType.DMA((3,)),
            ],
            compiler_params=pltpu.CompilerParams(
                collective_id=0, has_side_effects=True, vmem_limit_bytes=58 * 2**20
            ),
        )(
            positions,
            occupancy.reshape(tiles, LANES),
            bfactor.reshape(tiles, LANES),
            atom_type.reshape(tiles, LANES),
            miller,
            observed.reshape(1, LANES),
            weight.reshape(1, LANES),
            coef_a, coef_b, coef_c,
        )
        return gradient, residual.reshape(LANES)

    split = P(("atom", "refl"))
    return jax.shard_map(
        local,
        mesh=mesh,
        in_specs=(
            P(None, ("atom", "refl")), split, split, split,
            P(None, "refl"), P("refl"), P("refl"), P(), P(), P(),
        ),
        out_specs=(P(None, ("atom", "refl")), P("refl")),
        check_vma=False,
    )
```

```python
import functools
import math

import jax
import jax.numpy as jnp
from jax import lax
from jax.experimental import pallas as pl
from jax.experimental.pallas import tpu as pltpu
from jax.sharding import PartitionSpec as P

MESH = pl.DeviceIdType.MESH
two_pi = 6.283185307179586
cell_edge = 100.0
top = 48
TYPES, GAUSS = 8, 4
LANES = 128
unroll_b = 32


def rotate(ac, as_, bc, bs):
    return ac * bc - as_ * bs, ac * bs + as_ * bc


def kernel(
    n_atom, n_refl,
    pos_ref, occ_ref, bf_ref, type_ref, miller_ref, obs_ref, weight_ref, ca_ref, cb_ref, cc_ref,
    grad_ref, resid_ref,
    tx, ty, tz, store, form_rows, rows, idx_v, hs, ks, ls, folds, pairs, part, reduced, mine, total_in, every, plain,
    bu, bv, bh, bk, bl,
    g_send, g_recv, r_send, r_recv, a_send, a_recv, e_send, e_recv, i_sem, j_sem,
):
    me_a = lax.axis_index("atom")
    me_r = lax.axis_index("refl")
    tiles = occ_ref.shape[0]
    refl = n_refl * LANES
    half = LANES // 2
    picks = (hs, ks, ls)

    barrier = pltpu.get_barrier_semaphore()

    def greet(s, _):
        pl.semaphore_signal(barrier, inc=1, device_id=(me_a, lax.rem(me_r + s, n_refl)), device_id_type=MESH)
        return 0

    def greet_a(s, _):
        pl.semaphore_signal(barrier, inc=1, device_id=(lax.rem(me_a + s, n_atom), me_r), device_id_type=MESH)
        return 0

    lax.fori_loop(1, n_refl, greet, 0)
    lax.fori_loop(1, n_atom, greet_a, 0)

    rows[me_r] = miller_ref[...] + top
    own_rows = pl.ds(pl.multiple_of(me_r * LANES, LANES), LANES)
    own_idx = [pltpu.make_async_copy(rows.at[me_r, d], picks[d].at[own_rows], j_sem.at[d]) for d in range(3)]
    for copy in own_idx:
        copy.start()

    pl.semaphore_wait(barrier, n_refl - 1 + n_atom - 1)

    def to_refl(src, dst, send, recv, peer):
        return pltpu.make_async_remote_copy(
            src_ref=src, dst_ref=dst, send_sem=send, recv_sem=recv,
            device_id=(me_a, peer), device_id_type=MESH,
        )

    def all_of(ref, send, recv, count):
        part_of = ref.at[pl.ds(0, count)]
        return to_refl(part_of, part_of, send, recv, me_r)

    def g_start(s, _):
        to_refl(rows.at[me_r], rows.at[me_r], g_send, g_recv, lax.rem(me_r + s, n_refl)).start()
        return 0

    lax.fori_loop(1, n_refl, g_start, 0)

    first = []
    for d in range(3):
        x = jnp.concatenate([pos_ref[d : d + 1, a * LANES : (a + 1) * LANES] for a in range(tiles)], axis=0)
        turn = two_pi * (x - jnp.round(x))
        first.append((jnp.cos(turn), jnp.sin(turn)))
    decay = bf_ref[...] * (-0.25 / (cell_edge * cell_edge))
    occ = occ_ref[...]

    def table_step(m, carry):
        mf = m.astype(jnp.float32)
        damp = jnp.exp(decay * (mf * mf))
        after = []
        for d, table in enumerate((tx, ty, tz)):
            c, s = carry[2 * d], carry[2 * d + 1]
            scale = damp * occ if d == 2 else damp
            table[top + m, 0] = c * scale
            table[top + m, 1] = s * scale
            table[top - m, 0] = c * scale
            table[top - m, 1] = -(s * scale)
            after += list(rotate(c, s, *first[d]))
        return tuple(after)

    one = jnp.ones((tiles, LANES), jnp.float32)
    zero = jnp.zeros((tiles, LANES), jnp.float32)
    lax.fori_loop(0, top + 1, table_step, (one, zero) * 3)

    kind_row = lax.broadcasted_iota(jnp.int32, (TYPES, LANES), 0)

    def column(values):
        out = jnp.full((TYPES, LANES), values[0], jnp.float32)
        for t in range(1, TYPES):
            out = jnp.where(kind_row == t, values[t], out)
        return out

    size = [column([ca_ref[g, t] for t in range(TYPES)]) for g in range(GAUSS)]
    width = [column([-0.25 * cb_ref[g, t] for t in range(TYPES)]) for g in range(GAUSS)]
    level = column([cc_ref[t] for t in range(TYPES)])
    pad = jnp.zeros((LANES - TYPES, LANES), jnp.float32)

    def forms(b, where):
        s2 = jnp.zeros((TYPES, LANES), jnp.float32)
        for d in range(3):
            m = (jnp.broadcast_to(rows[b, d : d + 1, :], (TYPES, LANES)) - top).astype(jnp.float32)
            s2 = s2 + m * m
        s2 = s2 / (cell_edge * cell_edge)
        form = size[0] * jnp.exp(width[0] * s2)
        for g in range(1, GAUSS):
            form = form + size[g] * jnp.exp(width[g] * s2)
        form_rows[where, :] = jnp.concatenate([form + level, pad], axis=0).T

    forms(me_r, own_rows)
    folds[...] = jnp.zeros_like(folds)
    for copy in own_idx:
        copy.wait()

    kind = [type_ref[v * 8 : (v + 1) * 8, :] for v in range(tiles // 8)]

    def fold():
        for j in range(2):
            for g in range(half // 4):
                at = j * half * 8 + g * 32
                q = [folds[pl.ds(at + n, 8, stride=4), :] for n in range(4)]
                pairs[(j * half + g * 4) * 2 : (j * half + g * 4) * 2 + 8, :] = (q[0] + q[1]) + (q[2] + q[3])
        wide = [pairs[pl.ds(g * 16, 8, stride=2), :] + pairs[pl.ds(g * 16 + 1, 8, stride=2), :] for g in range(LANES // 8)]
        return jnp.sum(jnp.concatenate(wide, axis=0).T, axis=0, keepdims=True)

    def block_of(step):
        return lax.rem(me_r + n_refl - step, n_refl)

    def send_part(step):
        b = block_of(step)
        to_refl(part.at[b], reduced.at[me_r], r_send, r_recv, b).start()

    def chunk(n, _):
        @pl.when(n == 2)
        def _():
            all_of(rows, g_send, g_recv, n_refl - 1).wait_recv()
            for b in range(n_refl):
                for d in range(3):
                    idx_v[d, :, b * LANES : (b + 1) * LANES] = rows[b, d : d + 1, :]
            copies = [pltpu.make_async_copy(idx_v.at[d, 0], picks[d], i_sem.at[d]) for d in range(3)]
            for copy in copies:
                copy.start()
            for b in range(n_refl):
                forms(b, pl.ds(b * LANES, LANES))
            for copy in copies:
                copy.wait()

        part[block_of(lax.div(n + 1, 2) - 1), pl.ds(lax.rem(n + 1, 2), 1), :] = fold()
        r0 = block_of(lax.div(n, 2)) * LANES + lax.rem(n, 2) * half
        for u in range(half):
            r = r0 + u
            h, k, l = hs[r], ks[r], ls[r]
            form_row = jnp.broadcast_to(form_rows[pl.ds(r, 1), :], (8, LANES))
            real, imag = None, None
            for v in range(tiles // 8):
                off = v * 8
                c, s = rotate(
                    tx[h, 0, off : off + 8, :], tx[h, 1, off : off + 8, :],
                    ty[k, 0, off : off + 8, :], ty[k, 1, off : off + 8, :],
                )
                c, s = rotate(c, s, tz[l, 0, off : off + 8, :], tz[l, 1, off : off + 8, :])
                form = jnp.take_along_axis(form_row, kind[v], axis=1, mode="promise_in_bounds")
                c = c * form
                s = s * form
                store[r, 0, off : off + 8, :] = c
                store[r, 1, off : off + 8, :] = s
                real = c if real is None else real + c
                imag = s if imag is None else imag + s
            folds[u * 8 : u * 8 + 8, :] = real
            folds[(half + u) * 8 : (half + u) * 8 + 8, :] = imag

        @pl.when(jnp.logical_and(lax.rem(n, 2) == 0, n >= 4))
        def _():
            send_part(lax.div(n, 2) - 1)

        return 0

    lax.fori_loop(0, 2 * n_refl, chunk, 0)
    part[block_of(n_refl - 1), 1:2, :] = fold()
    send_part(n_refl - 1)
    reduced[me_r] = part[me_r]

    all_of(reduced, r_send, r_recv, n_refl - 1).wait_recv()
    mine[...] = jnp.sum(reduced[...], axis=0)
    total_in[me_a] = mine[...]

    def to_atom(src, dst, peer):
        return pltpu.make_async_remote_copy(
            src_ref=src, dst_ref=dst, send_sem=a_send, recv_sem=a_recv,
            device_id=(peer, me_r), device_id_type=MESH,
        )

    def a_start(s, _):
        to_atom(mine, total_in.at[me_a], lax.rem(me_a + s, n_atom)).start()
        return 0

    lax.fori_loop(1, n_atom, a_start, 0)

    for b in range(n_refl):
        for d, wide in enumerate((bh, bk, bl)):
            m = (rows[b, d : d + 1, :] - top).astype(jnp.float32)
            wide[b * LANES : (b + 1) * LANES, :] = jnp.broadcast_to(m, (LANES, LANES)).T

    rest_a = total_in.at[pl.ds(0, n_atom - 1)]
    to_atom(rest_a, rest_a, me_a).wait_recv()
    every[me_r, 0:2, :] = jnp.sum(total_in[...], axis=0)
    every[me_r, 2:3, :] = obs_ref[...]
    every[me_r, 3:4, :] = weight_ref[...]

    def e_start(s, _):
        to_refl(every.at[me_r], every.at[me_r], e_send, e_recv, lax.rem(me_r + s, n_refl)).start()
        return 0

    lax.fori_loop(1, n_refl, e_start, 0)
    all_of(every, e_send, e_recv, n_refl - 1).wait_recv()
    for b in range(n_refl):
        for q in range(4):
            plain[q * n_refl + b : q * n_refl + b + 1, :] = every[b, q : q + 1, :]
    first_half, second_half, obs, weight = (plain[q * n_refl : (q + 1) * n_refl, :] for q in range(4))

    atoms = tiles * LANES * n_atom * n_refl
    inv_atoms = 1.0 / math.sqrt(atoms)
    low = lax.broadcasted_iota(jnp.int32, (n_refl, LANES), 1) < half
    real_part = jnp.where(low, first_half, pltpu.roll(second_half, half, 1)) * inv_atoms
    imag_part = jnp.where(low, pltpu.roll(first_half, half, 1), second_half) * inv_atoms
    amp = jnp.sqrt(real_part * real_part + imag_part * imag_part + 0.25)
    over = jnp.sum(weight * obs * amp, axis=(0, 1), keepdims=True)
    under = jnp.sum(weight * amp * amp, axis=(0, 1), keepdims=True)
    scale = over / under
    resid = scale * amp - obs
    coeff = 2.0 * weight * scale * resid / (amp * math.sqrt(refl)) * (two_pi * inv_atoms)
    along_b = coeff * imag_part
    along_a = coeff * real_part
    plain[0:n_refl, :] = resid
    resid_ref[...] = plain[pl.ds(me_r, 1), :]
    for b in range(n_refl):
        bu[b * LANES : (b + 1) * LANES, :] = jnp.broadcast_to(along_b[b : b + 1, :], (LANES, LANES)).T
        bv[b * LANES : (b + 1) * LANES, :] = jnp.broadcast_to(along_a[b : b + 1, :], (LANES, LANES)).T

    def backward_chunk(i, acc):
        acc = [list(a) for a in acc]
        r0 = pl.multiple_of(i * unroll_b, unroll_b)
        for u in range(unroll_b):
            r = r0 + u
            wide = [jnp.broadcast_to(w[pl.ds(r, 1), :], (8, LANES)) for w in (bu, bv, bh, bk, bl)]
            for v in range(tiles // 8):
                off = v * 8
                inner = wide[0] * store[r, 0, off : off + 8, :] - wide[1] * store[r, 1, off : off + 8, :]
                for d in range(3):
                    acc[d][v] = acc[d][v] + wide[2 + d] * inner
        return tuple(tuple(a) for a in acc)

    none = jnp.zeros((8, LANES), jnp.float32)
    acc = lax.fori_loop(0, refl // unroll_b, backward_chunk, ((none,) * (tiles // 8),) * 3)
    for d in range(3):
        for v in range(tiles // 8):
            for a in range(8):
                t = v * 8 + a
                grad_ref[d : d + 1, t * LANES : (t + 1) * LANES] = acc[d][v][a : a + 1, :]

    all_of(rows, g_send, g_recv, n_refl - 1).wait_send()
    all_of(part, r_send, r_recv, n_refl - 1).wait_send()
    to_atom(rest_a, rest_a, me_a).wait_send()
    all_of(every, e_send, e_recv, n_refl - 1).wait_send()


def solution(mesh):
    n_atom, n_refl = mesh.shape["atom"], mesh.shape["refl"]

    def local(positions, occupancy, bfactor, atom_type, miller, observed, weight, coef_a, coef_b, coef_c):
        shard = positions.shape[1]
        tiles = shard // LANES
        refl = miller.shape[1] * n_refl
        vmem = pl.BlockSpec(memory_space=pltpu.VMEM)
        smem = pl.BlockSpec(memory_space=pltpu.SMEM)
        f32 = jnp.float32
        table = pltpu.VMEM((2 * top + 1, 2, tiles, LANES), f32)
        wide = pltpu.VMEM((refl, LANES), f32)
        pair_r = pltpu.VMEM((n_refl, 2, LANES), f32)
        smem_row = pltpu.SMEM((refl,), jnp.int32)
        dma = pltpu.SemaphoreType.DMA
        gradient, residual = pl.pallas_call(
            functools.partial(kernel, n_atom, n_refl),
            out_shape=(
                jax.ShapeDtypeStruct((3, shard), f32),
                jax.ShapeDtypeStruct((1, LANES), f32),
            ),
            in_specs=[vmem] * 7 + [smem] * 3,
            out_specs=(vmem, vmem),
            scratch_shapes=[
                table, table, table,
                pltpu.VMEM((refl, 2, tiles, LANES), f32),
                wide,
                pltpu.VMEM((n_refl, 3, LANES), jnp.int32),
                pltpu.VMEM((3, 1, refl), jnp.int32),
                smem_row, smem_row, smem_row,
                pltpu.VMEM((8 * LANES, LANES), f32),
                pltpu.VMEM((2 * LANES, LANES), f32),
                pair_r, pair_r,
                pltpu.VMEM((2, LANES), f32),
                pltpu.VMEM((n_atom, 2, LANES), f32),
                pltpu.VMEM((n_refl, 4, LANES), f32),
                pltpu.VMEM((4 * n_refl, LANES), f32),
                wide, wide, wide, wide, wide,
                dma, dma, dma, dma, dma, dma, dma, dma,
                dma((3,)), dma((3,)),
            ],
            compiler_params=pltpu.CompilerParams(
                collective_id=0, has_side_effects=True, vmem_limit_bytes=58 * 2**20
            ),
        )(
            positions,
            occupancy.reshape(tiles, LANES),
            bfactor.reshape(tiles, LANES),
            atom_type.reshape(tiles, LANES),
            miller,
            observed.reshape(1, LANES),
            weight.reshape(1, LANES),
            coef_a.T, coef_b.T, coef_c,
        )
        return gradient, residual.reshape(LANES)

    split = P(("atom", "refl"))
    return jax.shard_map(
        local,
        mesh=mesh,
        in_specs=(
            P(None, ("atom", "refl")), split, split, split,
            P(None, "refl"), P("refl"), P("refl"), P(), P(), P(),
        ),
        out_specs=(P(None, ("atom", "refl")), P("refl")),
        check_vma=False,
    )
```

```python
import functools
import math

import jax
import jax.numpy as jnp
from jax import lax
from jax.experimental import pallas as pl
from jax.experimental.pallas import tpu as pltpu
from jax.sharding import PartitionSpec as P

MESH = pl.DeviceIdType.MESH
two_pi = 6.283185307179586
cell_edge = 100.0
top = 48
TYPES, GAUSS = 8, 4
LANES = 128
unroll_b = 32


def rotate(ac, as_, bc, bs):
    return ac * bc - as_ * bs, ac * bs + as_ * bc


def kernel(
    n_atom, n_refl,
    pos_ref, occ_ref, bf_ref, type_ref, miller_ref, obs_ref, weight_ref, ca_ref, cb_ref, cc_ref,
    grad_ref, resid_ref,
    tx, ty, tz, store, form_rows, rows, idx_v, hs, ks, ls, folds, pairs, seen, ow, over_atom, over_refl,
    wide_a, wide_b, wide_1, wide_2, wide_h, wide_k, wide_l,
    g_send, g_recv, o_send, o_recv, a_send, a_recv, r_send, r_recv, i_sem,
):
    me_a = lax.axis_index("atom")
    me_r = lax.axis_index("refl")
    tiles = occ_ref.shape[0]
    refl = n_refl * LANES
    half = LANES // 2
    picks = (hs, ks, ls)

    barrier = pltpu.get_barrier_semaphore()

    def greet(s, _):
        pl.semaphore_signal(barrier, inc=1, device_id=(me_a, lax.rem(me_r + s, n_refl)), device_id_type=MESH)
        return 0

    def greet_a(s, _):
        pl.semaphore_signal(barrier, inc=1, device_id=(lax.rem(me_a + s, n_atom), me_r), device_id_type=MESH)
        return 0

    lax.fori_loop(1, n_refl, greet, 0)
    lax.fori_loop(1, n_atom, greet_a, 0)

    rows[me_r] = miller_ref[...] + top
    ow[me_r, 0:1, :] = obs_ref[...]
    ow[me_r, 1:2, :] = weight_ref[...]

    pl.semaphore_wait(barrier, n_refl - 1 + n_atom - 1)

    def to_refl(src, dst, send, recv, peer):
        return pltpu.make_async_remote_copy(
            src_ref=src, dst_ref=dst, send_sem=send, recv_sem=recv,
            device_id=(me_a, peer), device_id_type=MESH,
        )

    def all_of(ref, send, recv, count):
        part_of = ref.at[pl.ds(0, count)]
        return to_refl(part_of, part_of, send, recv, me_r)

    def g_start(s, _):
        to_refl(rows.at[me_r], rows.at[me_r], g_send, g_recv, lax.rem(me_r + s, n_refl)).start()
        return 0

    def o_start(s, _):
        to_refl(ow.at[me_r], ow.at[me_r], o_send, o_recv, lax.rem(me_r + s, n_refl)).start()
        return 0

    lax.fori_loop(1, n_refl, g_start, 0)
    lax.fori_loop(1, n_refl, o_start, 0)

    first = []
    for d in range(3):
        x = jnp.concatenate([pos_ref[d : d + 1, a * LANES : (a + 1) * LANES] for a in range(tiles)], axis=0)
        turn = two_pi * (x - jnp.round(x))
        first.append((jnp.cos(turn), jnp.sin(turn)))
    decay = bf_ref[...] * (-0.25 / (cell_edge * cell_edge))
    occ = occ_ref[...]

    def table_step(m, carry):
        mf = m.astype(jnp.float32)
        damp = jnp.exp(decay * (mf * mf))
        after = []
        for d, table in enumerate((tx, ty, tz)):
            c, s = carry[2 * d], carry[2 * d + 1]
            scale = damp * occ if d == 2 else damp
            table[top + m, 0] = c * scale
            table[top + m, 1] = s * scale
            table[top - m, 0] = c * scale
            table[top - m, 1] = -(s * scale)
            after += list(rotate(c, s, *first[d]))
        return tuple(after)

    one = jnp.ones((tiles, LANES), jnp.float32)
    zero = jnp.zeros((tiles, LANES), jnp.float32)
    lax.fori_loop(0, top + 1, table_step, (one, zero) * 3)

    kind_row = lax.broadcasted_iota(jnp.int32, (TYPES, LANES), 0)

    def column(values):
        out = jnp.full((TYPES, LANES), values[0], jnp.float32)
        for t in range(1, TYPES):
            out = jnp.where(kind_row == t, values[t], out)
        return out

    size = [column([ca_ref[g, t] for t in range(TYPES)]) for g in range(GAUSS)]
    width = [column([-0.25 * cb_ref[g, t] for t in range(TYPES)]) for g in range(GAUSS)]
    level = column([cc_ref[t] for t in range(TYPES)])
    pad = jnp.zeros((LANES - TYPES, LANES), jnp.float32)

    def forms(b, where):
        s2 = jnp.zeros((TYPES, LANES), jnp.float32)
        for d in range(3):
            m = (jnp.broadcast_to(rows[b, d : d + 1, :], (TYPES, LANES)) - top).astype(jnp.float32)
            s2 = s2 + m * m
        s2 = s2 / (cell_edge * cell_edge)
        form = size[0] * jnp.exp(width[0] * s2)
        for g in range(1, GAUSS):
            form = form + size[g] * jnp.exp(width[g] * s2)
        form_rows[where, :] = jnp.concatenate([form + level, pad], axis=0).T

    folds[...] = jnp.zeros_like(folds)
    kind = [type_ref[v * 8 : (v + 1) * 8, :] for v in range(tiles // 8)]

    ones = jnp.ones((8, LANES), jnp.bfloat16)

    def fold():
        for j in range(2):
            for g in range(half // 4):
                at = j * half * 8 + g * 32
                q = [folds[pl.ds(at + n, 8, stride=4), :] for n in range(4)]
                pairs[(j * half + g * 4) * 2 : (j * half + g * 4) * 2 + 8, :] = (q[0] + q[1]) + (q[2] + q[3])
        wide = [pairs[pl.ds(g * 16, 8, stride=2), :] + pairs[pl.ds(g * 16 + 1, 8, stride=2), :] for g in range(LANES // 8)]
        wide = jnp.concatenate(wide, axis=0)
        high = wide.astype(jnp.bfloat16)
        rest = (wide - high.astype(jnp.float32)).astype(jnp.bfloat16)
        lanes = (((1,), (1,)), ((), ()))
        total = lax.dot_general(ones, high, lanes, preferred_element_type=jnp.float32) + lax.dot_general(
            ones, rest, lanes, preferred_element_type=jnp.float32
        )
        return total[0:1, :]

    all_of(rows, g_send, g_recv, n_refl - 1).wait_recv()
    for b in range(n_refl):
        for d in range(3):
            idx_v[d, :, b * LANES : (b + 1) * LANES] = rows[b, d : d + 1, :]
    copies = [pltpu.make_async_copy(idx_v.at[d, 0], picks[d], i_sem.at[d]) for d in range(3)]
    for copy in copies:
        copy.start()
    for b in range(n_refl):
        forms(b, pl.ds(b * LANES, LANES))
    for copy in copies:
        copy.wait()

    steps = 2 * n_refl
    per = 8
    chunks = steps // per

    def to_atom(src, dst, q, peer):
        return pltpu.make_async_remote_copy(
            src_ref=src, dst_ref=dst, send_sem=a_send.at[q], recv_sem=a_recv.at[q],
            device_id=(peer, me_r), device_id_type=MESH,
        )

    def rest_atom(q):
        part_of = over_atom.at[q, pl.ds(0, n_atom - 1)]
        return to_atom(part_of, part_of, q, me_a)

    def rest_refl(q):
        part_of = over_refl.at[q, pl.ds(0, n_refl - 1)]
        return to_refl(part_of, part_of, r_send.at[q], r_recv.at[q], me_r)

    def send_atom(q):
        def one(s, _):
            mine = over_atom.at[q, me_a]
            to_atom(mine, mine, q, lax.rem(me_a + s, n_atom)).start()
            return 0

        lax.fori_loop(1, n_atom, one, 0)

    def send_refl(q):
        rest_atom(q).wait_recv()
        over_refl[q, me_r] = jnp.sum(over_atom[q], axis=0)

        def one(s, _):
            mine = over_refl.at[q, me_r]
            to_refl(mine, mine, r_send.at[q], r_recv.at[q], lax.rem(me_r + s, n_refl)).start()
            return 0

        lax.fori_loop(1, n_refl, one, 0)

    def forward_step(n, _):
        before = lax.rem(n + steps - 1, steps)
        over_atom[lax.div(before, per), me_a, pl.ds(lax.rem(before, per), 1), :] = fold()
        r0 = n * half
        for u in range(half):
            r = r0 + u
            h, k, l = hs[r], ks[r], ls[r]
            form_row = jnp.broadcast_to(form_rows[pl.ds(r, 1), :], (8, LANES))
            real, imag = None, None
            for v in range(tiles // 8):
                off = v * 8
                c, s = rotate(
                    tx[h, 0, off : off + 8, :], tx[h, 1, off : off + 8, :],
                    ty[k, 0, off : off + 8, :], ty[k, 1, off : off + 8, :],
                )
                c, s = rotate(c, s, tz[l, 0, off : off + 8, :], tz[l, 1, off : off + 8, :])
                form = jnp.take_along_axis(form_row, kind[v], axis=1, mode="promise_in_bounds")
                c = c * form
                s = s * form
                store[r, 0, off : off + 8, :] = c
                store[r, 1, off : off + 8, :] = s
                real = c if real is None else real + c
                imag = s if imag is None else imag + s
            folds[u * 8 : u * 8 + 8, :] = real
            folds[(half + u) * 8 : (half + u) * 8 + 8, :] = imag

        @pl.when(jnp.logical_and(lax.rem(n, per) == 0, n >= per))
        def _():
            send_atom(lax.div(n, per) - 1)

        return 0

    lax.fori_loop(0, steps, forward_step, 0)
    over_atom[chunks - 1, me_a, per - 1 : per, :] = fold()
    send_atom(chunks - 1)

    atoms = tiles * LANES * n_atom * n_refl
    inv_atoms = 1.0 / math.sqrt(atoms)
    factor = 2.0 / math.sqrt(refl)
    low = lax.broadcasted_iota(jnp.int32, (per, LANES), 1) < half

    def spread(row):
        return jnp.broadcast_to(row, (LANES, LANES)).T

    all_of(ow, o_send, o_recv, n_refl - 1).wait_recv()
    low_row = lax.broadcasted_iota(jnp.int32, (1, LANES), 1) < half
    for b in range(n_refl):
        for q in range(2):
            row = ow[b, q : q + 1, :]
            turned = pltpu.roll(row, half, 1)
            seen[q, 2 * b : 2 * b + 1, :] = jnp.where(low_row, row, turned)
            seen[q, 2 * b + 1 : 2 * b + 2, :] = jnp.where(low_row, turned, row)

    send_refl(0)
    for b in range(n_refl):
        for d, wide in enumerate((wide_h, wide_k, wide_l)):
            wide[b * LANES : (b + 1) * LANES, :] = spread((rows[b, d : d + 1, :] - top).astype(jnp.float32))
    send_refl(1)
    send_refl(2)

    def totals(q):
        rest_refl(q).wait_recv()
        both = jnp.sum(over_refl[q], axis=0) * inv_atoms
        square = both * both
        amp = jnp.sqrt(square + pltpu.roll(square, half, 1) + 0.25)
        return both, amp, seen[0, q * per : (q + 1) * per, :], seen[1, q * per : (q + 1) * per, :]

    def place(q, values, first, second):
        for i in range(per):
            at = (q * per + i) * half
            block = spread(values[i : i + 1, :])
            first[at : at + half, :] = block[:half]
            second[at : at + half, :] = block[half:]

    def both_sums(q, both, amp, obs, weight):
        place(q, both, wide_a, wide_b)
        place(q, jnp.where(low, factor * weight, factor * weight * obs / amp), wide_1, wide_2)

    def wide_rows(r, sources):
        return [jnp.broadcast_to(w[pl.ds(r, 1), :], (8, LANES)) for w in sources]

    def early(i, acc):
        acc = [[list(a) for a in g] for g in acc]
        r0 = i * unroll_b
        for u in range(unroll_b):
            r = r0 + u
            a, b, w1, w2, *m = wide_rows(r, (wide_a, wide_b, wide_1, wide_2, wide_h, wide_k, wide_l))
            for v in range(tiles // 8):
                off = v * 8
                p = b * store[r, 0, off : off + 8, :] - a * store[r, 1, off : off + 8, :]
                for g, w in enumerate((w1, w2)):
                    inner = w * p
                    for d in range(3):
                        acc[g][d][v] = acc[g][d][v] + m[d] * inner
        return tuple(tuple(tuple(a) for a in g) for g in acc)

    def late(i, acc):
        acc = [list(a) for a in acc]
        r0 = i * unroll_b
        for u in range(unroll_b):
            r = r0 + u
            a, b, *m = wide_rows(r, (wide_a, wide_b, wide_h, wide_k, wide_l))
            for v in range(tiles // 8):
                off = v * 8
                inner = b * store[r, 0, off : off + 8, :] - a * store[r, 1, off : off + 8, :]
                for d in range(3):
                    acc[d][v] = acc[d][v] + m[d] * inner
        return tuple(tuple(a) for a in acc)

    none = jnp.zeros((8, LANES), jnp.float32)
    group = ((none,) * (tiles // 8),) * 3
    size_q = per * half // unroll_b
    known = [totals(0)]
    both_sums(0, *known[0])
    acc2 = lax.fori_loop(0, size_q // 2, early, (group, group))
    send_refl(3)
    acc2 = lax.fori_loop(size_q // 2, size_q, early, acc2)
    known.append(totals(1))
    both_sums(1, *known[1])
    acc2 = lax.fori_loop(size_q, 2 * size_q, early, acc2)
    known += [totals(q) for q in range(2, chunks)]

    over = sum(jnp.where(low, weight * obs * amp, 0.0) for _, amp, obs, weight in known)
    under = sum(jnp.where(low, weight * amp * amp, 0.0) for _, amp, obs, weight in known)
    over = jnp.sum(over, axis=(0, 1), keepdims=True)
    under = jnp.sum(under, axis=(0, 1), keepdims=True)
    scale = over / under
    for q, (both, amp, obs, weight) in enumerate(known):
        seen[0, q * per : (q + 1) * per, :] = scale * amp
        if q >= 2:
            place(q, factor * weight * scale * (scale * amp - obs) / amp * both, wide_a, wide_b)
    acc = lax.fori_loop(2 * size_q, chunks * size_q, late, group)
    for d in range(3):
        for v in range(tiles // 8):
            total = acc[d][v] + scale * (scale * acc2[0][d][v] - acc2[1][d][v])
            for a in range(8):
                t = v * 8 + a
                grad_ref[d : d + 1, t * LANES : (t + 1) * LANES] = total[a : a + 1, :]
    resid_ref[...] = jnp.where(low_row, seen[0, pl.ds(2 * me_r, 1), :], seen[0, pl.ds(2 * me_r + 1, 1), :])

    all_of(rows, g_send, g_recv, n_refl - 1).wait_send()
    all_of(ow, o_send, o_recv, n_refl - 1).wait_send()
    for q in range(chunks):
        rest_atom(q).wait_send()
        rest_refl(q).wait_send()


def solution(mesh):
    n_atom, n_refl = mesh.shape["atom"], mesh.shape["refl"]

    def local(positions, occupancy, bfactor, atom_type, miller, observed, weight, coef_a, coef_b, coef_c):
        shard = positions.shape[1]
        tiles = shard // LANES
        refl = miller.shape[1] * n_refl
        vmem = pl.BlockSpec(memory_space=pltpu.VMEM)
        smem = pl.BlockSpec(memory_space=pltpu.SMEM)
        f32 = jnp.float32
        table = pltpu.VMEM((2 * top + 1, 2, tiles, LANES), f32)
        wide = pltpu.VMEM((refl, LANES), f32)
        smem_row = pltpu.SMEM((refl,), jnp.int32)
        dma = pltpu.SemaphoreType.DMA
        chunks = 2 * n_refl // 8
        gradient, residual = pl.pallas_call(
            functools.partial(kernel, n_atom, n_refl),
            out_shape=(
                jax.ShapeDtypeStruct((3, shard), f32),
                jax.ShapeDtypeStruct((1, LANES), f32),
            ),
            in_specs=[vmem] * 7 + [smem] * 3,
            out_specs=(vmem, vmem),
            scratch_shapes=[
                table, table, table,
                pltpu.VMEM((refl, 2, tiles, LANES), f32),
                wide,
                pltpu.VMEM((n_refl, 3, LANES), jnp.int32),
                pltpu.VMEM((3, 1, refl), jnp.int32),
                smem_row, smem_row, smem_row,
                pltpu.VMEM((8 * LANES, LANES), f32),
                pltpu.VMEM((2 * LANES, LANES), f32),
                pltpu.VMEM((2, 2 * n_refl, LANES), f32),
                pltpu.VMEM((n_refl, 2, LANES), f32),
                pltpu.VMEM((chunks, n_atom, 8, LANES), f32),
                pltpu.VMEM((chunks, n_refl, 8, LANES), f32),
                wide, wide, wide, wide, wide, wide, wide,
                dma, dma, dma, dma,
                dma((chunks,)), dma((chunks,)), dma((chunks,)), dma((chunks,)),
                dma((3,)),
            ],
            compiler_params=pltpu.CompilerParams(
                collective_id=0, has_side_effects=True, vmem_limit_bytes=58 * 2**20
            ),
        )(
            positions,
            occupancy.reshape(tiles, LANES),
            bfactor.reshape(tiles, LANES),
            atom_type.reshape(tiles, LANES),
            miller,
            observed.reshape(1, LANES),
            weight.reshape(1, LANES),
            coef_a.T, coef_b.T, coef_c,
        )
        inv_atoms = 1.0 / math.sqrt(shard * n_atom * n_refl)
        return gradient * (two_pi * inv_atoms), residual.reshape(LANES) - observed

    split = P(("atom", "refl"))
    return jax.shard_map(
        local,
        mesh=mesh,
        in_specs=(
            P(None, ("atom", "refl")), split, split, split,
            P(None, "refl"), P("refl"), P("refl"), P(), P(), P(),
        ),
        out_specs=(P(None, ("atom", "refl")), P("refl")),
        check_vma=False,
    )
```

```python
import functools
import math

import jax
import jax.numpy as jnp
from jax import lax
from jax.experimental import pallas as pl
from jax.experimental.pallas import tpu as pltpu
from jax.sharding import PartitionSpec as P

MESH = pl.DeviceIdType.MESH
two_pi = 6.283185307179586
cell_edge = 100.0
top = 48
TYPES, GAUSS = 8, 4
LANES = 128
SIDE = 4
unroll_b = 32


def rotate(ac, as_, bc, bs):
    return ac * bc - as_ * bs, ac * bs + as_ * bc


def kernel(
    n_atom, n_refl,
    pos_ref, occ_ref, bf_ref, type_ref, miller_ref, obs_ref, weight_ref, ca_ref, cb_ref, cc_ref,
    grad_ref, resid_ref,
    tx, ty, tz, store, form_rows, rows, idx_v, hs, ks, ls, folds, pairs, seen, ow, in_column, in_plane,
    wide_a, wide_b, wide_1, wide_2, wide_h, wide_k, wide_l,
    g_send, g_recv, o_send, o_recv, c_send, c_recv, p_send, p_recv, i_sem, j_sem,
):
    me_a = lax.axis_index("atom")
    me_r = lax.axis_index("refl")
    tiles = occ_ref.shape[0]
    refl = n_refl * LANES
    half = LANES // 2
    picks = (hs, ks, ls)

    x, zc = lax.div(me_a, SIDE), lax.rem(me_a, SIDE)
    z, y = lax.div(me_r, SIDE), lax.rem(me_r, SIDE)
    column = z * SIDE + zc
    plane = x * SIDE + y

    def column_peer(slot):
        return x * SIDE + lax.rem(slot, SIDE), lax.div(slot, SIDE) * SIDE + y

    def plane_peer(slot):
        return lax.div(slot, SIDE) * SIDE + zc, z * SIDE + lax.rem(slot, SIDE)

    barrier = pltpu.get_barrier_semaphore()

    def greet(peer):
        pl.semaphore_signal(barrier, inc=1, device_id=peer, device_id_type=MESH)

    def greet_far(i, _):
        turn, other = 1 + lax.div(i, SIDE), lax.rem(i, SIDE)
        greet(column_peer(other * SIDE + lax.rem(zc + turn, SIDE)))
        greet(plane_peer(lax.rem(x + turn, SIDE) * SIDE + other))
        return 0

    def greet_refl(s, _):
        greet((me_a, lax.rem(me_r + s, n_refl)))
        return 0

    far = SIDE * (SIDE - 1)
    lax.fori_loop(0, far, greet_far, 0)
    lax.fori_loop(1, n_refl, greet_refl, 0)

    rows[me_r] = miller_ref[...] + top
    ow[me_r, 0:1, :] = obs_ref[...]
    ow[me_r, 1:2, :] = weight_ref[...]
    own_rows = pl.ds(pl.multiple_of(me_r * LANES, LANES), LANES)
    own_idx = [pltpu.make_async_copy(rows.at[me_r, d], picks[d].at[own_rows], j_sem.at[d]) for d in range(3)]
    for copy in own_idx:
        copy.start()

    pl.semaphore_wait(barrier, n_refl - 1 + 2 * far)

    def to_refl(src, dst, send, recv, peer):
        return pltpu.make_async_remote_copy(
            src_ref=src, dst_ref=dst, send_sem=send, recv_sem=recv,
            device_id=(me_a, peer), device_id_type=MESH,
        )

    def all_of(ref, send, recv, count):
        part_of = ref.at[pl.ds(0, count)]
        return to_refl(part_of, part_of, send, recv, me_r)

    def g_start(s, _):
        to_refl(rows.at[me_r], rows.at[me_r], g_send, g_recv, lax.rem(me_r + s, n_refl)).start()
        return 0

    def o_start(s, _):
        to_refl(ow.at[me_r], ow.at[me_r], o_send, o_recv, lax.rem(me_r + s, n_refl)).start()
        return 0

    lax.fori_loop(1, n_refl, g_start, 0)
    lax.fori_loop(1, n_refl, o_start, 0)

    first = []
    for d in range(3):
        coord = jnp.concatenate([pos_ref[d : d + 1, a * LANES : (a + 1) * LANES] for a in range(tiles)], axis=0)
        turn = two_pi * (coord - jnp.round(coord))
        first.append((jnp.cos(turn), jnp.sin(turn)))
    decay = bf_ref[...] * (-0.25 / (cell_edge * cell_edge))
    occ = occ_ref[...]

    def table_step(m, carry):
        mf = m.astype(jnp.float32)
        damp = jnp.exp(decay * (mf * mf))
        after = []
        for d, table in enumerate((tx, ty, tz)):
            c, s = carry[2 * d], carry[2 * d + 1]
            scale = damp * occ if d == 2 else damp
            table[top + m, 0] = c * scale
            table[top + m, 1] = s * scale
            table[top - m, 0] = c * scale
            table[top - m, 1] = -(s * scale)
            after += list(rotate(c, s, *first[d]))
        return tuple(after)

    one = jnp.ones((tiles, LANES), jnp.float32)
    zero = jnp.zeros((tiles, LANES), jnp.float32)
    lax.fori_loop(0, top + 1, table_step, (one, zero) * 3)

    kind_row = lax.broadcasted_iota(jnp.int32, (TYPES, LANES), 0)

    def by_type(values):
        out = jnp.full((TYPES, LANES), values[0], jnp.float32)
        for t in range(1, TYPES):
            out = jnp.where(kind_row == t, values[t], out)
        return out

    size = [by_type([ca_ref[g, t] for t in range(TYPES)]) for g in range(GAUSS)]
    width = [by_type([-0.25 * cb_ref[g, t] for t in range(TYPES)]) for g in range(GAUSS)]
    level = by_type([cc_ref[t] for t in range(TYPES)])
    pad = jnp.zeros((LANES - TYPES, LANES), jnp.float32)

    def forms(b, where):
        s2 = jnp.zeros((TYPES, LANES), jnp.float32)
        for d in range(3):
            m = (jnp.broadcast_to(rows[b, d : d + 1, :], (TYPES, LANES)) - top).astype(jnp.float32)
            s2 = s2 + m * m
        s2 = s2 / (cell_edge * cell_edge)
        form = size[0] * jnp.exp(width[0] * s2)
        for g in range(1, GAUSS):
            form = form + size[g] * jnp.exp(width[g] * s2)
        form_rows[where, :] = jnp.concatenate([form + level, pad], axis=0).T

    forms(me_r, own_rows)
    folds[...] = jnp.zeros_like(folds)
    for copy in own_idx:
        copy.wait()
    kind = [type_ref[v * 8 : (v + 1) * 8, :] for v in range(tiles // 8)]

    ones = jnp.ones((8, LANES), jnp.bfloat16)

    def fold():
        for j in range(2):
            for g in range(half // 4):
                at = j * half * 8 + g * 32
                q = [folds[pl.ds(at + n, 8, stride=4), :] for n in range(4)]
                pairs[(j * half + g * 4) * 2 : (j * half + g * 4) * 2 + 8, :] = (q[0] + q[1]) + (q[2] + q[3])
        wide = [pairs[pl.ds(g * 16, 8, stride=2), :] + pairs[pl.ds(g * 16 + 1, 8, stride=2), :] for g in range(LANES // 8)]
        wide = jnp.concatenate(wide, axis=0)
        high = wide.astype(jnp.bfloat16)
        rest = (wide - high.astype(jnp.float32)).astype(jnp.bfloat16)
        lanes = (((1,), (1,)), ((), ()))
        total = lax.dot_general(ones, high, lanes, preferred_element_type=jnp.float32) + lax.dot_general(
            ones, rest, lanes, preferred_element_type=jnp.float32
        )
        return total[0:1, :]

    steps = 2 * n_refl
    per = 8
    chunks = steps // per

    def to_column(src, q, slot):
        return pltpu.make_async_remote_copy(
            src_ref=src, dst_ref=src, send_sem=c_send.at[q], recv_sem=c_recv.at[q],
            device_id=column_peer(slot), device_id_type=MESH,
        )

    def to_plane(src, q, slot):
        return pltpu.make_async_remote_copy(
            src_ref=src, dst_ref=src, send_sem=p_send.at[q], recv_sem=p_recv.at[q],
            device_id=plane_peer(slot), device_id_type=MESH,
        )

    peers = SIDE * SIDE

    def rest_column(q):
        return to_column(in_column.at[q, pl.ds(0, peers - 1)], q, column)

    def rest_plane(q):
        return to_plane(in_plane.at[q, pl.ds(0, peers - 1)], q, plane)

    def send_column(q):
        def one(s, _):
            to_column(in_column.at[q, column], q, lax.rem(column + s, peers)).start()
            return 0

        lax.fori_loop(1, peers, one, 0)

    def send_plane(q):
        rest_column(q).wait_recv()
        in_plane[q, plane] = jnp.sum(in_column[q], axis=0)

        def one(s, _):
            to_plane(in_plane.at[q, plane], q, lax.rem(plane + s, peers)).start()
            return 0

        lax.fori_loop(1, peers, one, 0)

    def step_at(i):
        later = i - 2
        return jnp.where(i < 2, 2 * me_r + i, jnp.where(later < 2 * me_r, later, i))

    def prepare():
        all_of(rows, g_send, g_recv, n_refl - 1).wait_recv()
        for b in range(n_refl):
            for d in range(3):
                idx_v[d, :, b * LANES : (b + 1) * LANES] = rows[b, d : d + 1, :]
        copies = [pltpu.make_async_copy(idx_v.at[d, 0], picks[d], i_sem.at[d]) for d in range(3)]
        for copy in copies:
            copy.start()
        for b in range(n_refl):
            forms(b, pl.ds(b * LANES, LANES))
        for copy in copies:
            copy.wait()

    def forward_step(i, _):
        @pl.when(i == 2)
        def _():
            prepare()

        n = step_at(i)
        before = step_at(lax.rem(i + steps - 1, steps))
        in_column[lax.div(before, per), column, pl.ds(lax.rem(before, per), 1), :] = fold()
        r0 = n * half
        for u in range(half):
            r = r0 + u
            h, k, l = hs[r], ks[r], ls[r]
            form_row = jnp.broadcast_to(form_rows[pl.ds(r, 1), :], (8, LANES))
            real, imag = None, None
            for v in range(tiles // 8):
                off = v * 8
                c, s = rotate(
                    tx[h, 0, off : off + 8, :], tx[h, 1, off : off + 8, :],
                    ty[k, 0, off : off + 8, :], ty[k, 1, off : off + 8, :],
                )
                c, s = rotate(c, s, tz[l, 0, off : off + 8, :], tz[l, 1, off : off + 8, :])
                form = jnp.take_along_axis(form_row, kind[v], axis=1, mode="promise_in_bounds")
                c = c * form
                s = s * form
                store[r, 0, off : off + 8, :] = c
                store[r, 1, off : off + 8, :] = s
                real = c if real is None else real + c
                imag = s if imag is None else imag + s
            folds[u * 8 : u * 8 + 8, :] = real
            folds[(half + u) * 8 : (half + u) * 8 + 8, :] = imag

        @pl.when(jnp.logical_and(i > 2, lax.div(n, per) > lax.div(before, per)))
        def _():
            send_column(lax.div(before, per))

        return 0

    lax.fori_loop(0, steps, forward_step, 0)
    last = step_at(steps - 1)
    in_column[chunks - 1, column, pl.ds(lax.rem(last, per), 1), :] = fold()
    send_column(chunks - 1)

    atoms = tiles * LANES * n_atom * n_refl
    inv_atoms = 1.0 / math.sqrt(atoms)
    factor = 2.0 / math.sqrt(refl)
    low = lax.broadcasted_iota(jnp.int32, (per, LANES), 1) < half

    def spread(row):
        return jnp.broadcast_to(row, (LANES, LANES)).T

    all_of(ow, o_send, o_recv, n_refl - 1).wait_recv()
    low_row = lax.broadcasted_iota(jnp.int32, (1, LANES), 1) < half
    for b in range(n_refl):
        for q in range(2):
            row = ow[b, q : q + 1, :]
            turned = pltpu.roll(row, half, 1)
            seen[q, 2 * b : 2 * b + 1, :] = jnp.where(low_row, row, turned)
            seen[q, 2 * b + 1 : 2 * b + 2, :] = jnp.where(low_row, turned, row)

    send_plane(0)
    for b in range(n_refl):
        for d, wide in enumerate((wide_h, wide_k, wide_l)):
            wide[b * LANES : (b + 1) * LANES, :] = spread((rows[b, d : d + 1, :] - top).astype(jnp.float32))
    send_plane(1)
    send_plane(2)

    def totals(q):
        rest_plane(q).wait_recv()
        both = jnp.sum(in_plane[q], axis=0) * inv_atoms
        square = both * both
        amp = jnp.sqrt(square + pltpu.roll(square, half, 1) + 0.25)
        return both, amp, seen[0, q * per : (q + 1) * per, :], seen[1, q * per : (q + 1) * per, :]

    def place(q, values, first, second):
        for i in range(per):
            at = (q * per + i) * half
            block = spread(values[i : i + 1, :])
            first[at : at + half, :] = block[:half]
            second[at : at + half, :] = block[half:]

    def both_sums(q, both, amp, obs, weight):
        place(q, both, wide_a, wide_b)
        place(q, jnp.where(low, factor * weight, factor * weight * obs / amp), wide_1, wide_2)

    def wide_rows(r, sources):
        return [jnp.broadcast_to(w[pl.ds(r, 1), :], (8, LANES)) for w in sources]

    def early(i, acc):
        acc = [[list(a) for a in g] for g in acc]
        r0 = i * unroll_b
        for u in range(unroll_b):
            r = r0 + u
            a, b, w1, w2, *m = wide_rows(r, (wide_a, wide_b, wide_1, wide_2, wide_h, wide_k, wide_l))
            for v in range(tiles // 8):
                off = v * 8
                p = b * store[r, 0, off : off + 8, :] - a * store[r, 1, off : off + 8, :]
                for g, w in enumerate((w1, w2)):
                    inner = w * p
                    for d in range(3):
                        acc[g][d][v] = acc[g][d][v] + m[d] * inner
        return tuple(tuple(tuple(a) for a in g) for g in acc)

    def late(i, acc):
        acc = [list(a) for a in acc]
        r0 = i * unroll_b
        for u in range(unroll_b):
            r = r0 + u
            a, b, *m = wide_rows(r, (wide_a, wide_b, wide_h, wide_k, wide_l))
            for v in range(tiles // 8):
                off = v * 8
                inner = b * store[r, 0, off : off + 8, :] - a * store[r, 1, off : off + 8, :]
                for d in range(3):
                    acc[d][v] = acc[d][v] + m[d] * inner
        return tuple(tuple(a) for a in acc)

    none = jnp.zeros((8, LANES), jnp.float32)
    group = ((none,) * (tiles // 8),) * 3
    size_q = per * half // unroll_b
    known = [totals(0)]
    both_sums(0, *known[0])
    acc2 = lax.fori_loop(0, size_q // 4, early, (group, group))
    send_plane(3)
    acc2 = lax.fori_loop(size_q // 4, size_q, early, acc2)
    known.append(totals(1))
    both_sums(1, *known[1])
    acc2 = lax.fori_loop(size_q, 2 * size_q, early, acc2)
    known += [totals(q) for q in range(2, chunks)]

    over = sum(jnp.where(low, weight * obs * amp, 0.0) for _, amp, obs, weight in known)
    under = sum(jnp.where(low, weight * amp * amp, 0.0) for _, amp, obs, weight in known)
    over = jnp.sum(over, axis=(0, 1), keepdims=True)
    under = jnp.sum(under, axis=(0, 1), keepdims=True)
    scale = over / under
    for q, (both, amp, obs, weight) in enumerate(known):
        seen[0, q * per : (q + 1) * per, :] = scale * amp
        if q >= 2:
            place(q, factor * weight * scale * (scale * amp - obs) / amp * both, wide_a, wide_b)
    acc = lax.fori_loop(2 * size_q, chunks * size_q, late, group)
    for d in range(3):
        for v in range(tiles // 8):
            total = acc[d][v] + scale * (scale * acc2[0][d][v] - acc2[1][d][v])
            for a in range(8):
                t = v * 8 + a
                grad_ref[d : d + 1, t * LANES : (t + 1) * LANES] = total[a : a + 1, :]
    resid_ref[...] = jnp.where(low_row, seen[0, pl.ds(2 * me_r, 1), :], seen[0, pl.ds(2 * me_r + 1, 1), :])

    all_of(rows, g_send, g_recv, n_refl - 1).wait_send()
    all_of(ow, o_send, o_recv, n_refl - 1).wait_send()
    for q in range(chunks):
        rest_column(q).wait_send()
        rest_plane(q).wait_send()


def solution(mesh):
    n_atom, n_refl = mesh.shape["atom"], mesh.shape["refl"]

    def local(positions, occupancy, bfactor, atom_type, miller, observed, weight, coef_a, coef_b, coef_c):
        shard = positions.shape[1]
        tiles = shard // LANES
        refl = miller.shape[1] * n_refl
        vmem = pl.BlockSpec(memory_space=pltpu.VMEM)
        smem = pl.BlockSpec(memory_space=pltpu.SMEM)
        f32 = jnp.float32
        table = pltpu.VMEM((2 * top + 1, 2, tiles, LANES), f32)
        wide = pltpu.VMEM((refl, LANES), f32)
        smem_row = pltpu.SMEM((refl,), jnp.int32)
        dma = pltpu.SemaphoreType.DMA
        chunks = 2 * n_refl // 8
        gradient, residual = pl.pallas_call(
            functools.partial(kernel, n_atom, n_refl),
            out_shape=(
                jax.ShapeDtypeStruct((3, shard), f32),
                jax.ShapeDtypeStruct((1, LANES), f32),
            ),
            in_specs=[vmem] * 7 + [smem] * 3,
            out_specs=(vmem, vmem),
            scratch_shapes=[
                table, table, table,
                pltpu.VMEM((refl, 2, tiles, LANES), f32),
                wide,
                pltpu.VMEM((n_refl, 3, LANES), jnp.int32),
                pltpu.VMEM((3, 1, refl), jnp.int32),
                smem_row, smem_row, smem_row,
                pltpu.VMEM((8 * LANES, LANES), f32),
                pltpu.VMEM((2 * LANES, LANES), f32),
                pltpu.VMEM((2, 2 * n_refl, LANES), f32),
                pltpu.VMEM((n_refl, 2, LANES), f32),
                pltpu.VMEM((chunks, SIDE * SIDE, 8, LANES), f32),
                pltpu.VMEM((chunks, SIDE * SIDE, 8, LANES), f32),
                wide, wide, wide, wide, wide, wide, wide,
                dma, dma, dma, dma,
                dma((chunks,)), dma((chunks,)), dma((chunks,)), dma((chunks,)),
                dma((3,)), dma((3,)),
            ],
            compiler_params=pltpu.CompilerParams(
                collective_id=0, has_side_effects=True, vmem_limit_bytes=58 * 2**20
            ),
        )(
            positions,
            occupancy.reshape(tiles, LANES),
            bfactor.reshape(tiles, LANES),
            atom_type.reshape(tiles, LANES),
            miller,
            observed.reshape(1, LANES),
            weight.reshape(1, LANES),
            coef_a.T, coef_b.T, coef_c,
        )
        inv_atoms = 1.0 / math.sqrt(shard * n_atom * n_refl)
        return gradient * (two_pi * inv_atoms), residual.reshape(LANES) - observed

    split = P(("atom", "refl"))
    return jax.shard_map(
        local,
        mesh=mesh,
        in_specs=(
            P(None, ("atom", "refl")), split, split, split,
            P(None, "refl"), P("refl"), P("refl"), P(), P(), P(),
        ),
        out_specs=(P(None, ("atom", "refl")), P("refl")),
        check_vma=False,
    )
```

```python
import functools
import math

import jax
import jax.numpy as jnp
from jax import lax
from jax.experimental import pallas as pl
from jax.experimental.pallas import tpu as pltpu
from jax.sharding import PartitionSpec as P

MESH = pl.DeviceIdType.MESH
two_pi = 6.283185307179586
cell_edge = 100.0
top = 48
TYPES, GAUSS = 8, 4
LANES = 128
SIDE = 4
unroll_b = 32


def rotate(ac, as_, bc, bs):
    return ac * bc - as_ * bs, ac * bs + as_ * bc


def kernel(n_atom, n_refl, *refs):
    sources, (grad_ref, resid_ref), inputs, rest = refs[:10], refs[10:12], refs[12:22], refs[22:]
    pos_ref, occ_ref, bf_ref, type_ref, miller_ref, obs_ref, weight_ref, ca_ref, cb_ref, cc_ref = inputs
    (
        tx, ty, tz, store, form_rows, rows, idx_v, hs, ks, ls, folds, pairs, seen, ow, in_column, in_plane,
        wide_a, wide_b, wide_1, wide_2, wide_h, wide_k, wide_l,
        g_send, g_recv, o_send, o_recv, c_send, c_recv, p_send, p_recv, i_sem, j_sem, in_sem,
    ) = rest
    me_a = lax.axis_index("atom")
    me_r = lax.axis_index("refl")
    tiles = occ_ref.shape[0]
    refl = n_refl * LANES
    half = LANES // 2
    picks = (hs, ks, ls)

    x, zc = lax.div(me_a, SIDE), lax.rem(me_a, SIDE)
    z, y = lax.div(me_r, SIDE), lax.rem(me_r, SIDE)
    column = z * SIDE + zc
    plane = x * SIDE + y

    def column_peer(slot):
        return x * SIDE + lax.rem(slot, SIDE), lax.div(slot, SIDE) * SIDE + y

    def plane_peer(slot):
        return lax.div(slot, SIDE) * SIDE + zc, z * SIDE + lax.rem(slot, SIDE)

    barrier = pltpu.get_barrier_semaphore()

    def greet(peer):
        pl.semaphore_signal(barrier, inc=1, device_id=peer, device_id_type=MESH)

    def greet_far(i, _):
        turn, other = 1 + lax.div(i, SIDE), lax.rem(i, SIDE)
        greet(column_peer(other * SIDE + lax.rem(zc + turn, SIDE)))
        greet(plane_peer(lax.rem(x + turn, SIDE) * SIDE + other))
        return 0

    def greet_refl(s, _):
        greet((me_a, lax.rem(me_r + s, n_refl)))
        return 0

    far = SIDE * (SIDE - 1)
    lax.fori_loop(1, n_refl, greet_refl, 0)
    arrive = [pltpu.make_async_copy(src, dst, in_sem.at[n]) for n, (src, dst) in enumerate(zip(sources, inputs))]
    for copy in arrive:
        copy.start()
    lax.fori_loop(0, far, greet_far, 0)
    for copy in arrive:
        copy.wait()

    rows[me_r] = miller_ref[...] + top
    ow[me_r, 0:1, :] = obs_ref[...]
    ow[me_r, 1:2, :] = weight_ref[...]
    own_rows = pl.ds(pl.multiple_of(me_r * LANES, LANES), LANES)
    own_idx = [pltpu.make_async_copy(rows.at[me_r, d], picks[d].at[own_rows], j_sem.at[d]) for d in range(3)]
    for copy in own_idx:
        copy.start()

    pl.semaphore_wait(barrier, n_refl - 1 + 2 * far)

    def to_refl(src, dst, send, recv, peer):
        return pltpu.make_async_remote_copy(
            src_ref=src, dst_ref=dst, send_sem=send, recv_sem=recv,
            device_id=(me_a, peer), device_id_type=MESH,
        )

    def all_of(ref, send, recv, count):
        part_of = ref.at[pl.ds(0, count)]
        return to_refl(part_of, part_of, send, recv, me_r)

    def g_start(s, _):
        to_refl(rows.at[me_r], rows.at[me_r], g_send, g_recv, lax.rem(me_r + s, n_refl)).start()
        return 0

    def o_start(s, _):
        to_refl(ow.at[me_r], ow.at[me_r], o_send, o_recv, lax.rem(me_r + s, n_refl)).start()
        return 0

    lax.fori_loop(1, n_refl, g_start, 0)
    lax.fori_loop(1, n_refl, o_start, 0)

    first = []
    for d in range(3):
        coord = jnp.concatenate([pos_ref[d : d + 1, a * LANES : (a + 1) * LANES] for a in range(tiles)], axis=0)
        turn = two_pi * (coord - jnp.round(coord))
        first.append((jnp.cos(turn), jnp.sin(turn)))
    decay = bf_ref[...] * (-0.25 / (cell_edge * cell_edge))
    occ = occ_ref[...]

    def table_step(m, carry):
        mf = m.astype(jnp.float32)
        damp = jnp.exp(decay * (mf * mf))
        after = []
        for d, table in enumerate((tx, ty, tz)):
            c, s = carry[2 * d], carry[2 * d + 1]
            scale = damp * occ if d == 2 else damp
            table[top + m, 0] = c * scale
            table[top + m, 1] = s * scale
            table[top - m, 0] = c * scale
            table[top - m, 1] = -(s * scale)
            after += list(rotate(c, s, *first[d]))
        return tuple(after)

    one = jnp.ones((tiles, LANES), jnp.float32)
    zero = jnp.zeros((tiles, LANES), jnp.float32)
    lax.fori_loop(0, top + 1, table_step, (one, zero) * 3)

    kind_row = lax.broadcasted_iota(jnp.int32, (TYPES, LANES), 0)

    def by_type(values):
        out = jnp.full((TYPES, LANES), values[0], jnp.float32)
        for t in range(1, TYPES):
            out = jnp.where(kind_row == t, values[t], out)
        return out

    size = [by_type([ca_ref[g, t] for t in range(TYPES)]) for g in range(GAUSS)]
    width = [by_type([-0.25 * cb_ref[g, t] for t in range(TYPES)]) for g in range(GAUSS)]
    level = by_type([cc_ref[t] for t in range(TYPES)])
    pad = jnp.zeros((LANES - TYPES, LANES), jnp.float32)

    def forms(b, where):
        s2 = jnp.zeros((TYPES, LANES), jnp.float32)
        for d in range(3):
            m = (jnp.broadcast_to(rows[b, d : d + 1, :], (TYPES, LANES)) - top).astype(jnp.float32)
            s2 = s2 + m * m
        s2 = s2 / (cell_edge * cell_edge)
        form = size[0] * jnp.exp(width[0] * s2)
        for g in range(1, GAUSS):
            form = form + size[g] * jnp.exp(width[g] * s2)
        form_rows[where, :] = jnp.concatenate([form + level, pad], axis=0).T

    forms(me_r, own_rows)
    folds[...] = jnp.zeros_like(folds)
    for copy in own_idx:
        copy.wait()
    kind = [type_ref[v * 8 : (v + 1) * 8, :] for v in range(tiles // 8)]

    ones = jnp.ones((8, LANES), jnp.bfloat16)

    def fold():
        for j in range(2):
            for g in range(half // 4):
                at = j * half * 8 + g * 32
                q = [folds[pl.ds(at + n, 8, stride=4), :] for n in range(4)]
                pairs[(j * half + g * 4) * 2 : (j * half + g * 4) * 2 + 8, :] = (q[0] + q[1]) + (q[2] + q[3])
        wide = [pairs[pl.ds(g * 16, 8, stride=2), :] + pairs[pl.ds(g * 16 + 1, 8, stride=2), :] for g in range(LANES // 8)]
        wide = jnp.concatenate(wide, axis=0)
        high = wide.astype(jnp.bfloat16)
        rest = (wide - high.astype(jnp.float32)).astype(jnp.bfloat16)
        lanes = (((1,), (1,)), ((), ()))
        total = lax.dot_general(ones, high, lanes, preferred_element_type=jnp.float32) + lax.dot_general(
            ones, rest, lanes, preferred_element_type=jnp.float32
        )
        return total[0:1, :]

    steps = 2 * n_refl
    per = 8
    chunks = steps // per
    hand_on = steps - 6

    def to_column(src, q, slot):
        return pltpu.make_async_remote_copy(
            src_ref=src, dst_ref=src, send_sem=c_send.at[q], recv_sem=c_recv.at[q],
            device_id=column_peer(slot), device_id_type=MESH,
        )

    def to_plane(src, q, slot):
        return pltpu.make_async_remote_copy(
            src_ref=src, dst_ref=src, send_sem=p_send.at[q], recv_sem=p_recv.at[q],
            device_id=plane_peer(slot), device_id_type=MESH,
        )

    peers = SIDE * SIDE

    def rest_column(q):
        return to_column(in_column.at[q, pl.ds(0, peers - 1)], q, column)

    def rest_plane(q):
        return to_plane(in_plane.at[q, pl.ds(0, peers - 1)], q, plane)

    def send_column(q):
        def one(s, _):
            to_column(in_column.at[q, column], q, lax.rem(column + s, peers)).start()
            return 0

        lax.fori_loop(1, peers, one, 0)

    def send_plane(q):
        rest_column(q).wait_recv()
        in_plane[q, plane] = jnp.sum(in_column[q], axis=0)

        def one(s, _):
            to_plane(in_plane.at[q, plane], q, lax.rem(plane + s, peers)).start()
            return 0

        lax.fori_loop(1, peers, one, 0)

    def step_at(i):
        later = i - 2
        return jnp.where(i < 2, 2 * me_r + i, jnp.where(later < 2 * me_r, later, i))

    def picks_copies():
        return [pltpu.make_async_copy(idx_v.at[d, 0], picks[d], i_sem.at[d]) for d in range(3)]

    def prepare():
        all_of(rows, g_send, g_recv, n_refl - 1).wait_recv()
        for b in range(n_refl):
            for d in range(3):
                idx_v[d, :, b * LANES : (b + 1) * LANES] = rows[b, d : d + 1, :]
        for copy in picks_copies():
            copy.start()
        for b in range(n_refl):
            forms(b, pl.ds(b * LANES, LANES))

    def forward_step(i, _):
        @pl.when(i == 2)
        def _():
            prepare()
            for copy in picks_copies():
                copy.wait()

        @pl.when(i == hand_on)
        def _():
            send_plane(0)

        n = step_at(i)
        before = step_at(lax.rem(i + steps - 1, steps))
        in_column[lax.div(before, per), column, pl.ds(lax.rem(before, per), 1), :] = fold()
        r0 = n * half
        for u in range(half):
            r = r0 + u
            h, k, l = hs[r], ks[r], ls[r]
            form_row = jnp.broadcast_to(form_rows[pl.ds(r, 1), :], (8, LANES))
            real, imag = None, None
            for v in range(tiles // 8):
                off = v * 8
                c, s = rotate(
                    tx[h, 0, off : off + 8, :], tx[h, 1, off : off + 8, :],
                    ty[k, 0, off : off + 8, :], ty[k, 1, off : off + 8, :],
                )
                c, s = rotate(c, s, tz[l, 0, off : off + 8, :], tz[l, 1, off : off + 8, :])
                form = jnp.take_along_axis(form_row, kind[v], axis=1, mode="promise_in_bounds")
                c = c * form
                s = s * form
                store[r, 0, off : off + 8, :] = c
                store[r, 1, off : off + 8, :] = s
                real = c if real is None else real + c
                imag = s if imag is None else imag + s
            folds[u * 8 : u * 8 + 8, :] = real
            folds[(half + u) * 8 : (half + u) * 8 + 8, :] = imag

        @pl.when(jnp.logical_and(i > 2, lax.div(n, per) > lax.div(before, per)))
        def _():
            send_column(lax.div(before, per))

        return 0

    lax.fori_loop(0, steps, forward_step, 0)
    last = step_at(steps - 1)
    in_column[chunks - 1, column, pl.ds(lax.rem(last, per), 1), :] = fold()
    send_column(chunks - 1)

    atoms = tiles * LANES * n_atom * n_refl
    inv_atoms = 1.0 / math.sqrt(atoms)
    factor = 2.0 / math.sqrt(refl)
    low = lax.broadcasted_iota(jnp.int32, (per, LANES), 1) < half

    def spread(row):
        return jnp.broadcast_to(row, (LANES, LANES)).T

    all_of(ow, o_send, o_recv, n_refl - 1).wait_recv()
    low_row = lax.broadcasted_iota(jnp.int32, (1, LANES), 1) < half
    for b in range(n_refl):
        for q in range(2):
            row = ow[b, q : q + 1, :]
            turned = pltpu.roll(row, half, 1)
            seen[q, 2 * b : 2 * b + 1, :] = jnp.where(low_row, row, turned)
            seen[q, 2 * b + 1 : 2 * b + 2, :] = jnp.where(low_row, turned, row)

    send_plane(1)
    for b in range(n_refl):
        for d, wide in enumerate((wide_h, wide_k, wide_l)):
            wide[b * LANES : (b + 1) * LANES, :] = spread((rows[b, d : d + 1, :] - top).astype(jnp.float32))
    send_plane(2)

    def totals(q):
        rest_plane(q).wait_recv()
        both = jnp.sum(in_plane[q], axis=0) * inv_atoms
        square = both * both
        amp = jnp.sqrt(square + pltpu.roll(square, half, 1) + 0.25)
        return both, amp, seen[0, q * per : (q + 1) * per, :], seen[1, q * per : (q + 1) * per, :]

    def place(q, values, first, second):
        for i in range(per):
            at = (q * per + i) * half
            block = spread(values[i : i + 1, :])
            first[at : at + half, :] = block[:half]
            second[at : at + half, :] = block[half:]

    def both_sums(q, both, amp, obs, weight):
        place(q, both, wide_a, wide_b)
        place(q, jnp.where(low, factor * weight, factor * weight * obs / amp), wide_1, wide_2)

    def wide_rows(r, sources):
        return [jnp.broadcast_to(w[pl.ds(r, 1), :], (8, LANES)) for w in sources]

    def early(i, acc):
        acc = [[list(a) for a in g] for g in acc]
        r0 = i * unroll_b
        for u in range(unroll_b):
            r = r0 + u
            a, b, w1, w2, *m = wide_rows(r, (wide_a, wide_b, wide_1, wide_2, wide_h, wide_k, wide_l))
            for v in range(tiles // 8):
                off = v * 8
                p = b * store[r, 0, off : off + 8, :] - a * store[r, 1, off : off + 8, :]
                for g, w in enumerate((w1, w2)):
                    inner = w * p
                    for d in range(3):
                        acc[g][d][v] = acc[g][d][v] + m[d] * inner
        return tuple(tuple(tuple(a) for a in g) for g in acc)

    def late(i, acc):
        acc = [list(a) for a in acc]
        r0 = i * unroll_b
        for u in range(unroll_b):
            r = r0 + u
            a, b, *m = wide_rows(r, (wide_a, wide_b, wide_h, wide_k, wide_l))
            for v in range(tiles // 8):
                off = v * 8
                inner = b * store[r, 0, off : off + 8, :] - a * store[r, 1, off : off + 8, :]
                for d in range(3):
                    acc[d][v] = acc[d][v] + m[d] * inner
        return tuple(tuple(a) for a in acc)

    none = jnp.zeros((8, LANES), jnp.float32)
    group = ((none,) * (tiles // 8),) * 3
    size_q = per * half // unroll_b
    known = []
    acc2 = (group, group)
    for q in range(chunks - 1):
        known.append(totals(q))
        both_sums(q, *known[q])
        acc2 = lax.fori_loop(q * size_q, (q + 1) * size_q, early, acc2)
        if q == 0:
            send_plane(chunks - 1)
    known.append(totals(chunks - 1))

    over = sum(jnp.where(low, weight * obs * amp, 0.0) for _, amp, obs, weight in known)
    under = sum(jnp.where(low, weight * amp * amp, 0.0) for _, amp, obs, weight in known)
    over = jnp.sum(over, axis=(0, 1), keepdims=True)
    under = jnp.sum(under, axis=(0, 1), keepdims=True)
    scale = over / under
    for q, (both, amp, obs, weight) in enumerate(known):
        seen[0, q * per : (q + 1) * per, :] = scale * amp
        if q == chunks - 1:
            place(q, factor * weight * scale * (scale * amp - obs) / amp * both, wide_a, wide_b)
    acc = lax.fori_loop((chunks - 1) * size_q, chunks * size_q, late, group)
    for d in range(3):
        for v in range(tiles // 8):
            total = acc[d][v] + scale * (scale * acc2[0][d][v] - acc2[1][d][v])
            for a in range(8):
                t = v * 8 + a
                grad_ref[d : d + 1, t * LANES : (t + 1) * LANES] = total[a : a + 1, :]
    resid_ref[...] = jnp.where(low_row, seen[0, pl.ds(2 * me_r, 1), :], seen[0, pl.ds(2 * me_r + 1, 1), :])

    all_of(rows, g_send, g_recv, n_refl - 1).wait_send()
    all_of(ow, o_send, o_recv, n_refl - 1).wait_send()
    for q in range(chunks):
        rest_column(q).wait_send()
        rest_plane(q).wait_send()


def solution(mesh):
    n_atom, n_refl = mesh.shape["atom"], mesh.shape["refl"]

    def local(positions, occupancy, bfactor, atom_type, miller, observed, weight, coef_a, coef_b, coef_c):
        shard = positions.shape[1]
        tiles = shard // LANES
        refl = miller.shape[1] * n_refl
        vmem = pl.BlockSpec(memory_space=pltpu.VMEM)
        f32 = jnp.float32
        table = pltpu.VMEM((2 * top + 1, 2, tiles, LANES), f32)
        wide = pltpu.VMEM((refl, LANES), f32)
        smem_row = pltpu.SMEM((refl,), jnp.int32)
        dma = pltpu.SemaphoreType.DMA
        chunks = 2 * n_refl // 8
        gradient, residual = pl.pallas_call(
            functools.partial(kernel, n_atom, n_refl),
            out_shape=(
                pltpu.VMEM((3, shard), f32),
                pltpu.VMEM((1, LANES), f32),
            ),
            in_specs=[pl.BlockSpec(memory_space=pl.ANY)] * 10,
            out_specs=(vmem, vmem),
            scratch_shapes=[
                pltpu.VMEM((3, shard), f32),
                pltpu.VMEM((tiles, LANES), f32),
                pltpu.VMEM((tiles, LANES), f32),
                pltpu.VMEM((tiles, LANES), jnp.int32),
                pltpu.VMEM((3, LANES), jnp.int32),
                pltpu.VMEM((1, LANES), f32),
                pltpu.VMEM((1, LANES), f32),
                pltpu.SMEM((GAUSS, TYPES), f32),
                pltpu.SMEM((GAUSS, TYPES), f32),
                pltpu.SMEM((TYPES,), f32),
                table, table, table,
                pltpu.VMEM((refl, 2, tiles, LANES), f32),
                wide,
                pltpu.VMEM((n_refl, 3, LANES), jnp.int32),
                pltpu.VMEM((3, 1, refl), jnp.int32),
                smem_row, smem_row, smem_row,
                pltpu.VMEM((8 * LANES, LANES), f32),
                pltpu.VMEM((2 * LANES, LANES), f32),
                pltpu.VMEM((2, 2 * n_refl, LANES), f32),
                pltpu.VMEM((n_refl, 2, LANES), f32),
                pltpu.VMEM((chunks, SIDE * SIDE, 8, LANES), f32),
                pltpu.VMEM((chunks, SIDE * SIDE, 8, LANES), f32),
                wide, wide, wide, wide, wide, wide, wide,
                dma, dma, dma, dma,
                dma((chunks,)), dma((chunks,)), dma((chunks,)), dma((chunks,)),
                dma((3,)), dma((3,)), dma((10,)),
            ],
            compiler_params=pltpu.CompilerParams(
                collective_id=0, has_side_effects=True, vmem_limit_bytes=58 * 2**20
            ),
        )(
            positions,
            occupancy.reshape(tiles, LANES),
            bfactor.reshape(tiles, LANES),
            atom_type.reshape(tiles, LANES),
            miller,
            observed.reshape(1, LANES),
            weight.reshape(1, LANES),
            coef_a.T, coef_b.T, coef_c,
        )
        inv_atoms = 1.0 / math.sqrt(shard * n_atom * n_refl)
        return gradient * (two_pi * inv_atoms), residual.reshape(LANES) - observed

    split = P(("atom", "refl"))
    return jax.shard_map(
        local,
        mesh=mesh,
        in_specs=(
            P(None, ("atom", "refl")), split, split, split,
            P(None, "refl"), P("refl"), P("refl"), P(), P(), P(),
        ),
        out_specs=(P(None, ("atom", "refl")), P("refl")),
        check_vma=False,
    )
```

```python
import functools
import math

import jax
import jax.numpy as jnp
from jax import lax
from jax.experimental import pallas as pl
from jax.experimental.pallas import tpu as pltpu
from jax.sharding import PartitionSpec as P

MESH = pl.DeviceIdType.MESH
two_pi = 6.283185307179586
cell_edge = 100.0
top = 48
TYPES, GAUSS = 8, 4
LANES = 128
SIDE = 4
unroll_b = 32


def rotate(ac, as_, bc, bs):
    return ac * bc - as_ * bs, ac * bs + as_ * bc


def kernel(n_atom, n_refl, *refs):
    sources, (grad_ref, resid_ref), inputs, rest = refs[:10], refs[10:12], refs[12:22], refs[22:]
    pos_ref, occ_ref, bf_ref, type_ref, miller_ref, obs_ref, weight_ref, ca_ref, cb_ref, cc_ref = inputs
    (
        tx, ty, tz, store, form_rows, rows, idx_v, hs, ks, ls, folds, pairs, seen, ow, in_column, in_plane,
        wide_a, wide_b, wide_1, wide_2, wide_h, wide_k, wide_l,
        g_send, g_recv, o_send, o_recv, c_send, c_recv, p_send, p_recv, i_sem, j_sem, in_sem,
    ) = rest
    me_a = lax.axis_index("atom")
    me_r = lax.axis_index("refl")
    tiles = occ_ref.shape[0]
    refl = n_refl * LANES
    half = LANES // 2
    picks = (hs, ks, ls)

    x, zc = lax.div(me_a, SIDE), lax.rem(me_a, SIDE)
    z, y = lax.div(me_r, SIDE), lax.rem(me_r, SIDE)
    column = z * SIDE + zc
    plane = x * SIDE + y

    xs, zcs, zs, ys = ([lax.rem(at + turn, SIDE) for turn in range(SIDE)] for at in (x, zc, z, y))
    turns = [(i, j) for i in range(SIDE) for j in range(SIDE) if i or j]
    refl_peers = [(me_a, zs[i] * SIDE + ys[j]) for i, j in turns]
    column_peers = [(x * SIDE + zcs[j], zs[i] * SIDE + y) for i, j in turns]
    plane_peers = [(xs[i] * SIDE + zc, z * SIDE + ys[j]) for i, j in turns]

    barrier = pltpu.get_barrier_semaphore()

    def greet(peer):
        pl.semaphore_signal(barrier, inc=1, device_id=peer, device_id_type=MESH)

    far = SIDE * (SIDE - 1)
    for peer in refl_peers:
        greet(peer)
    arrive = [pltpu.make_async_copy(src, dst, in_sem.at[n]) for n, (src, dst) in enumerate(zip(sources, inputs))]
    for copy in arrive:
        copy.start()
    for (i, j), over_column, over_plane in zip(turns, column_peers, plane_peers):
        if j:
            greet(over_column)
        if i:
            greet(over_plane)
    for copy in arrive:
        copy.wait()

    rows[me_r] = miller_ref[...] + top
    ow[me_r, 0:1, :] = obs_ref[...]
    ow[me_r, 1:2, :] = weight_ref[...]
    own_rows = pl.ds(pl.multiple_of(me_r * LANES, LANES), LANES)
    own_idx = [pltpu.make_async_copy(rows.at[me_r, d], picks[d].at[own_rows], j_sem.at[d]) for d in range(3)]
    for copy in own_idx:
        copy.start()

    pl.semaphore_wait(barrier, n_refl - 1 + 2 * far)

    def to_refl(src, send, recv, peer):
        return pltpu.make_async_remote_copy(
            src_ref=src, dst_ref=src, send_sem=send, recv_sem=recv, device_id=peer, device_id_type=MESH
        )

    def all_of(ref, send, recv, count):
        return to_refl(ref.at[pl.ds(0, count)], send, recv, refl_peers[0])

    for peer in refl_peers:
        to_refl(rows.at[me_r], g_send, g_recv, peer).start()
    for peer in refl_peers:
        to_refl(ow.at[me_r], o_send, o_recv, peer).start()

    first = []
    for d in range(3):
        coord = jnp.concatenate([pos_ref[d : d + 1, a * LANES : (a + 1) * LANES] for a in range(tiles)], axis=0)
        turn = two_pi * (coord - jnp.round(coord))
        first.append((jnp.cos(turn), jnp.sin(turn)))
    decay = bf_ref[...] * (-0.25 / (cell_edge * cell_edge))
    occ = occ_ref[...]

    def table_step(m, carry):
        mf = m.astype(jnp.float32)
        damp = jnp.exp(decay * (mf * mf))
        after = []
        for d, table in enumerate((tx, ty, tz)):
            c, s = carry[2 * d], carry[2 * d + 1]
            scale = damp * occ if d == 2 else damp
            table[top + m, 0] = c * scale
            table[top + m, 1] = s * scale
            table[top - m, 0] = c * scale
            table[top - m, 1] = -(s * scale)
            after += list(rotate(c, s, *first[d]))
        return tuple(after)

    one = jnp.ones((tiles, LANES), jnp.float32)
    zero = jnp.zeros((tiles, LANES), jnp.float32)
    lax.fori_loop(0, top + 1, table_step, (one, zero) * 3)

    kind_row = lax.broadcasted_iota(jnp.int32, (TYPES, LANES), 0)

    def by_type(values):
        out = jnp.full((TYPES, LANES), values[0], jnp.float32)
        for t in range(1, TYPES):
            out = jnp.where(kind_row == t, values[t], out)
        return out

    size = [by_type([ca_ref[g, t] for t in range(TYPES)]) for g in range(GAUSS)]
    width = [by_type([-0.25 * cb_ref[g, t] for t in range(TYPES)]) for g in range(GAUSS)]
    level = by_type([cc_ref[t] for t in range(TYPES)])
    pad = jnp.zeros((LANES - TYPES, LANES), jnp.float32)

    def forms(b, where):
        s2 = jnp.zeros((TYPES, LANES), jnp.float32)
        for d in range(3):
            m = (jnp.broadcast_to(rows[b, d : d + 1, :], (TYPES, LANES)) - top).astype(jnp.float32)
            s2 = s2 + m * m
        s2 = s2 / (cell_edge * cell_edge)
        form = size[0] * jnp.exp(width[0] * s2)
        for g in range(1, GAUSS):
            form = form + size[g] * jnp.exp(width[g] * s2)
        form_rows[where, :] = jnp.concatenate([form + level, pad], axis=0).T

    forms(me_r, own_rows)
    folds[...] = jnp.zeros_like(folds)
    for copy in own_idx:
        copy.wait()
    kind = [type_ref[v * 8 : (v + 1) * 8, :] for v in range(tiles // 8)]

    ones = jnp.ones((8, LANES), jnp.bfloat16)

    def fold():
        for j in range(2):
            for g in range(half // 4):
                at = j * half * 8 + g * 32
                q = [folds[pl.ds(at + n, 8, stride=4), :] for n in range(4)]
                pairs[(j * half + g * 4) * 2 : (j * half + g * 4) * 2 + 8, :] = (q[0] + q[1]) + (q[2] + q[3])
        wide = [pairs[pl.ds(g * 16, 8, stride=2), :] + pairs[pl.ds(g * 16 + 1, 8, stride=2), :] for g in range(LANES // 8)]
        wide = jnp.concatenate(wide, axis=0)
        high = wide.astype(jnp.bfloat16)
        rest = (wide - high.astype(jnp.float32)).astype(jnp.bfloat16)
        lanes = (((1,), (1,)), ((), ()))
        total = lax.dot_general(ones, high, lanes, preferred_element_type=jnp.float32) + lax.dot_general(
            ones, rest, lanes, preferred_element_type=jnp.float32
        )
        return total[0:1, :]

    steps = 2 * n_refl
    per = 8
    chunks = steps // per
    hand_on = steps - 6

    def to_column(src, q, peer):
        return pltpu.make_async_remote_copy(
            src_ref=src, dst_ref=src, send_sem=c_send.at[q], recv_sem=c_recv.at[q],
            device_id=peer, device_id_type=MESH,
        )

    def to_plane(src, q, peer):
        return pltpu.make_async_remote_copy(
            src_ref=src, dst_ref=src, send_sem=p_send.at[q], recv_sem=p_recv.at[q],
            device_id=peer, device_id_type=MESH,
        )

    def rest_column(q):
        return to_column(in_column.at[q, pl.ds(0, len(turns))], q, column_peers[0])

    def rest_plane(q):
        return to_plane(in_plane.at[q, pl.ds(0, len(turns))], q, plane_peers[0])

    def send_column(q):
        for peer in column_peers:
            to_column(in_column.at[q, column], q, peer).start()

    def send_plane(q):
        rest_column(q).wait_recv()
        in_plane[q, plane] = jnp.sum(in_column[q], axis=0)
        for peer in plane_peers:
            to_plane(in_plane.at[q, plane], q, peer).start()

    def step_at(i):
        later = i - 2
        return jnp.where(i < 2, 2 * me_r + i, jnp.where(later < 2 * me_r, later, i))

    def picks_copies():
        return [pltpu.make_async_copy(idx_v.at[d, 0], picks[d], i_sem.at[d]) for d in range(3)]

    def prepare():
        all_of(rows, g_send, g_recv, n_refl - 1).wait_recv()
        for b in range(n_refl):
            for d in range(3):
                idx_v[d, :, b * LANES : (b + 1) * LANES] = rows[b, d : d + 1, :]
        for copy in picks_copies():
            copy.start()
        for b in range(n_refl):
            forms(b, pl.ds(b * LANES, LANES))

    def forward_step(i, _):
        @pl.when(i == 2)
        def _():
            prepare()
            for copy in picks_copies():
                copy.wait()

        @pl.when(i == hand_on)
        def _():
            send_plane(0)

        n = step_at(i)
        before = step_at(lax.rem(i + steps - 1, steps))
        in_column[lax.div(before, per), column, pl.ds(lax.rem(before, per), 1), :] = fold()
        r0 = n * half
        for u in range(half):
            r = r0 + u
            h, k, l = hs[r], ks[r], ls[r]
            form_row = jnp.broadcast_to(form_rows[pl.ds(r, 1), :], (8, LANES))
            real, imag = None, None
            for v in range(tiles // 8):
                off = v * 8
                c, s = rotate(
                    tx[h, 0, off : off + 8, :], tx[h, 1, off : off + 8, :],
                    ty[k, 0, off : off + 8, :], ty[k, 1, off : off + 8, :],
                )
                c, s = rotate(c, s, tz[l, 0, off : off + 8, :], tz[l, 1, off : off + 8, :])
                form = jnp.take_along_axis(form_row, kind[v], axis=1, mode="promise_in_bounds")
                c = c * form
                s = s * form
                store[r, 0, off : off + 8, :] = c
                store[r, 1, off : off + 8, :] = s
                real = c if real is None else real + c
                imag = s if imag is None else imag + s
            folds[u * 8 : u * 8 + 8, :] = real
            folds[(half + u) * 8 : (half + u) * 8 + 8, :] = imag

        @pl.when(jnp.logical_and(i > 2, lax.div(n, per) > lax.div(before, per)))
        def _():
            send_column(lax.div(before, per))

        return 0

    lax.fori_loop(0, steps, forward_step, 0)
    last = step_at(steps - 1)
    in_column[chunks - 1, column, pl.ds(lax.rem(last, per), 1), :] = fold()
    send_column(chunks - 1)

    atoms = tiles * LANES * n_atom * n_refl
    inv_atoms = 1.0 / math.sqrt(atoms)
    factor = 2.0 / math.sqrt(refl)
    low = lax.broadcasted_iota(jnp.int32, (per, LANES), 1) < half

    def spread(row):
        return jnp.broadcast_to(row, (LANES, LANES)).T

    all_of(ow, o_send, o_recv, n_refl - 1).wait_recv()
    low_row = lax.broadcasted_iota(jnp.int32, (1, LANES), 1) < half
    for b in range(n_refl):
        for q in range(2):
            row = ow[b, q : q + 1, :]
            turned = pltpu.roll(row, half, 1)
            seen[q, 2 * b : 2 * b + 1, :] = jnp.where(low_row, row, turned)
            seen[q, 2 * b + 1 : 2 * b + 2, :] = jnp.where(low_row, turned, row)

    send_plane(1)
    for b in range(n_refl):
        for d, wide in enumerate((wide_h, wide_k, wide_l)):
            wide[b * LANES : (b + 1) * LANES, :] = spread((rows[b, d : d + 1, :] - top).astype(jnp.float32))
    send_plane(2)

    def totals(q):
        rest_plane(q).wait_recv()
        both = jnp.sum(in_plane[q], axis=0) * inv_atoms
        square = both * both
        amp = jnp.sqrt(square + pltpu.roll(square, half, 1) + 0.25)
        return both, amp, seen[0, q * per : (q + 1) * per, :], seen[1, q * per : (q + 1) * per, :]

    def place(q, values, first, second):
        for i in range(per):
            at = (q * per + i) * half
            block = spread(values[i : i + 1, :])
            first[at : at + half, :] = block[:half]
            second[at : at + half, :] = block[half:]

    def both_sums(q, both, amp, obs, weight):
        place(q, both, wide_a, wide_b)
        place(q, jnp.where(low, factor * weight, factor * weight * obs / amp), wide_1, wide_2)

    def wide_rows(r, sources):
        return [jnp.broadcast_to(w[pl.ds(r, 1), :], (8, LANES)) for w in sources]

    def early(i, acc):
        acc = [[list(a) for a in g] for g in acc]
        r0 = i * unroll_b
        for u in range(unroll_b):
            r = r0 + u
            a, b, w1, w2, *m = wide_rows(r, (wide_a, wide_b, wide_1, wide_2, wide_h, wide_k, wide_l))
            for v in range(tiles // 8):
                off = v * 8
                p = b * store[r, 0, off : off + 8, :] - a * store[r, 1, off : off + 8, :]
                for g, w in enumerate((w1, w2)):
                    inner = w * p
                    for d in range(3):
                        acc[g][d][v] = acc[g][d][v] + m[d] * inner
        return tuple(tuple(tuple(a) for a in g) for g in acc)

    def late(i, acc):
        acc = [list(a) for a in acc]
        r0 = i * unroll_b
        for u in range(unroll_b):
            r = r0 + u
            a, b, *m = wide_rows(r, (wide_a, wide_b, wide_h, wide_k, wide_l))
            for v in range(tiles // 8):
                off = v * 8
                inner = b * store[r, 0, off : off + 8, :] - a * store[r, 1, off : off + 8, :]
                for d in range(3):
                    acc[d][v] = acc[d][v] + m[d] * inner
        return tuple(tuple(a) for a in acc)

    none = jnp.zeros((8, LANES), jnp.float32)
    group = ((none,) * (tiles // 8),) * 3
    size_q = per * half // unroll_b
    known = []
    acc2 = (group, group)
    for q in range(chunks - 1):
        known.append(totals(q))
        both_sums(q, *known[q])
        acc2 = lax.fori_loop(q * size_q, (q + 1) * size_q, early, acc2)
        if q == 0:
            send_plane(chunks - 1)
    known.append(totals(chunks - 1))

    over = sum(jnp.where(low, weight * obs * amp, 0.0) for _, amp, obs, weight in known)
    under = sum(jnp.where(low, weight * amp * amp, 0.0) for _, amp, obs, weight in known)
    over = jnp.sum(over, axis=(0, 1), keepdims=True)
    under = jnp.sum(under, axis=(0, 1), keepdims=True)
    scale = over / under
    for q, (both, amp, obs, weight) in enumerate(known):
        seen[0, q * per : (q + 1) * per, :] = scale * amp
        if q == chunks - 1:
            place(q, factor * weight * scale * (scale * amp - obs) / amp * both, wide_a, wide_b)
    acc = lax.fori_loop((chunks - 1) * size_q, chunks * size_q, late, group)
    for d in range(3):
        for v in range(tiles // 8):
            total = acc[d][v] + scale * (scale * acc2[0][d][v] - acc2[1][d][v])
            for a in range(8):
                t = v * 8 + a
                grad_ref[d : d + 1, t * LANES : (t + 1) * LANES] = total[a : a + 1, :]
    resid_ref[...] = jnp.where(low_row, seen[0, pl.ds(2 * me_r, 1), :], seen[0, pl.ds(2 * me_r + 1, 1), :])

    all_of(rows, g_send, g_recv, n_refl - 1).wait_send()
    all_of(ow, o_send, o_recv, n_refl - 1).wait_send()
    for q in range(chunks):
        rest_column(q).wait_send()
        rest_plane(q).wait_send()


def solution(mesh):
    n_atom, n_refl = mesh.shape["atom"], mesh.shape["refl"]

    def local(positions, occupancy, bfactor, atom_type, miller, observed, weight, coef_a, coef_b, coef_c):
        shard = positions.shape[1]
        tiles = shard // LANES
        refl = miller.shape[1] * n_refl
        vmem = pl.BlockSpec(memory_space=pltpu.VMEM)
        f32 = jnp.float32
        table = pltpu.VMEM((2 * top + 1, 2, tiles, LANES), f32)
        wide = pltpu.VMEM((refl, LANES), f32)
        smem_row = pltpu.SMEM((refl,), jnp.int32)
        dma = pltpu.SemaphoreType.DMA
        chunks = 2 * n_refl // 8
        gradient, residual = pl.pallas_call(
            functools.partial(kernel, n_atom, n_refl),
            out_shape=(
                pltpu.VMEM((3, shard), f32),
                pltpu.VMEM((1, LANES), f32),
            ),
            in_specs=[pl.BlockSpec(memory_space=pl.ANY)] * 10,
            out_specs=(vmem, vmem),
            scratch_shapes=[
                pltpu.VMEM((3, shard), f32),
                pltpu.VMEM((tiles, LANES), f32),
                pltpu.VMEM((tiles, LANES), f32),
                pltpu.VMEM((tiles, LANES), jnp.int32),
                pltpu.VMEM((3, LANES), jnp.int32),
                pltpu.VMEM((1, LANES), f32),
                pltpu.VMEM((1, LANES), f32),
                pltpu.SMEM((GAUSS, TYPES), f32),
                pltpu.SMEM((GAUSS, TYPES), f32),
                pltpu.SMEM((TYPES,), f32),
                table, table, table,
                pltpu.VMEM((refl, 2, tiles, LANES), f32),
                wide,
                pltpu.VMEM((n_refl, 3, LANES), jnp.int32),
                pltpu.VMEM((3, 1, refl), jnp.int32),
                smem_row, smem_row, smem_row,
                pltpu.VMEM((8 * LANES, LANES), f32),
                pltpu.VMEM((2 * LANES, LANES), f32),
                pltpu.VMEM((2, 2 * n_refl, LANES), f32),
                pltpu.VMEM((n_refl, 2, LANES), f32),
                pltpu.VMEM((chunks, SIDE * SIDE, 8, LANES), f32),
                pltpu.VMEM((chunks, SIDE * SIDE, 8, LANES), f32),
                wide, wide, wide, wide, wide, wide, wide,
                dma, dma, dma, dma,
                dma((chunks,)), dma((chunks,)), dma((chunks,)), dma((chunks,)),
                dma((3,)), dma((3,)), dma((10,)),
            ],
            compiler_params=pltpu.CompilerParams(
                collective_id=0, has_side_effects=True, vmem_limit_bytes=58 * 2**20
            ),
        )(
            positions,
            occupancy.reshape(tiles, LANES),
            bfactor.reshape(tiles, LANES),
            atom_type.reshape(tiles, LANES),
            miller,
            observed.reshape(1, LANES),
            weight.reshape(1, LANES),
            coef_a.T, coef_b.T, coef_c,
        )
        inv_atoms = 1.0 / math.sqrt(shard * n_atom * n_refl)
        return gradient * (two_pi * inv_atoms), residual.reshape(LANES) - observed

    split = P(("atom", "refl"))
    return jax.shard_map(
        local,
        mesh=mesh,
        in_specs=(
            P(None, ("atom", "refl")), split, split, split,
            P(None, "refl"), P("refl"), P("refl"), P(), P(), P(),
        ),
        out_specs=(P(None, ("atom", "refl")), P("refl")),
        check_vma=False,
    )
```

```python
import functools
import math

import jax
import jax.numpy as jnp
from jax import lax
from jax.experimental import pallas as pl
from jax.experimental.pallas import tpu as pltpu
from jax.sharding import PartitionSpec as P

MESH = pl.DeviceIdType.MESH
two_pi = 6.283185307179586
cell_edge = 100.0
top = 48
TYPES, GAUSS = 8, 4
LANES = 128
SIDE = 4
unroll_b = 32


def rotate(ac, as_, bc, bs):
    return ac * bc - as_ * bs, ac * bs + as_ * bc


def kernel(n_atom, n_refl, *refs):
    sources, (grad_ref, resid_ref), inputs, rest = refs[:10], refs[10:12], refs[12:22], refs[22:]
    pos_ref, occ_ref, bf_ref, type_ref, miller_ref, obs_ref, weight_ref, ca_ref, cb_ref, cc_ref = inputs
    (
        tx, ty, tz, store, form_rows, rows, idx_v, hs, ks, ls, folds, pairs, seen, ow, in_column, in_plane,
        wide_a, wide_b, wide_1, wide_2, wide_h, wide_k, wide_l,
        g_send, g_recv, o_send, o_recv, c_send, c_recv, p_send, p_recv, i_sem, j_sem, in_sem,
    ) = rest
    me_a = lax.axis_index("atom")
    me_r = lax.axis_index("refl")
    tiles = occ_ref.shape[0]
    refl = n_refl * LANES
    half = LANES // 2
    picks = (hs, ks, ls)

    x, zc = lax.div(me_a, SIDE), lax.rem(me_a, SIDE)
    z, y = lax.div(me_r, SIDE), lax.rem(me_r, SIDE)
    column = z * SIDE + zc
    plane = x * SIDE + y

    xs, zcs, zs, ys = ([lax.rem(at + turn, SIDE) for turn in range(SIDE)] for at in (x, zc, z, y))
    turns = [(i, j) for i in range(SIDE) for j in range(SIDE) if i or j]
    refl_peers = [(me_a, zs[i] * SIDE + ys[j]) for i, j in turns]
    column_peers = [(x * SIDE + zcs[j], zs[i] * SIDE + y) for i, j in turns]
    plane_peers = [(xs[i] * SIDE + zc, z * SIDE + ys[j]) for i, j in turns]

    barrier = pltpu.get_barrier_semaphore()

    def greet(peer):
        pl.semaphore_signal(barrier, inc=1, device_id=peer, device_id_type=MESH)

    far = SIDE * (SIDE - 1)
    for peer in refl_peers:
        greet(peer)
    arrive = [pltpu.make_async_copy(src, dst, in_sem.at[n]) for n, (src, dst) in enumerate(zip(sources, inputs))]
    for copy in arrive:
        copy.start()
    for (i, j), over_column, over_plane in zip(turns, column_peers, plane_peers):
        if j:
            greet(over_column)
        if i:
            greet(over_plane)
    for copy in arrive:
        copy.wait()

    rows[me_r] = miller_ref[...] + top
    ow[me_r, 0:1, :] = obs_ref[...]
    ow[me_r, 1:2, :] = weight_ref[...]
    own_rows = pl.ds(pl.multiple_of(me_r * LANES, LANES), LANES)
    own_idx = [pltpu.make_async_copy(rows.at[me_r, d], picks[d].at[own_rows], j_sem.at[d]) for d in range(3)]
    for copy in own_idx:
        copy.start()

    pl.semaphore_wait(barrier, n_refl - 1 + 2 * far)

    def to_refl(src, send, recv, peer):
        return pltpu.make_async_remote_copy(
            src_ref=src, dst_ref=src, send_sem=send, recv_sem=recv, device_id=peer, device_id_type=MESH
        )

    def all_of(ref, send, recv, count):
        return to_refl(ref.at[pl.ds(0, count)], send, recv, refl_peers[0])

    for peer in refl_peers:
        to_refl(rows.at[me_r], g_send, g_recv, peer).start()
    first = []
    for d in range(3):
        coord = jnp.concatenate([pos_ref[d : d + 1, a * LANES : (a + 1) * LANES] for a in range(tiles)], axis=0)
        turn = two_pi * (coord - jnp.round(coord))
        first.append((jnp.cos(turn), jnp.sin(turn)))
    decay = bf_ref[...] * (-0.25 / (cell_edge * cell_edge))
    occ = occ_ref[...]

    def table_step(m, carry):
        mf = m.astype(jnp.float32)
        damp = jnp.exp(decay * (mf * mf))
        after = []
        for d, table in enumerate((tx, ty, tz)):
            c, s = carry[2 * d], carry[2 * d + 1]
            scale = damp * occ if d == 2 else damp
            table[top + m, 0] = c * scale
            table[top + m, 1] = s * scale
            table[top - m, 0] = c * scale
            table[top - m, 1] = -(s * scale)
            after += list(rotate(c, s, *first[d]))
        return tuple(after)

    one = jnp.ones((tiles, LANES), jnp.float32)
    zero = jnp.zeros((tiles, LANES), jnp.float32)
    lax.fori_loop(0, top + 1, table_step, (one, zero) * 3)

    for peer in refl_peers:
        to_refl(ow.at[me_r], o_send, o_recv, peer).start()

    kind_row = lax.broadcasted_iota(jnp.int32, (TYPES, LANES), 0)

    def by_type(values):
        out = jnp.full((TYPES, LANES), values[0], jnp.float32)
        for t in range(1, TYPES):
            out = jnp.where(kind_row == t, values[t], out)
        return out

    size = [by_type([ca_ref[g, t] for t in range(TYPES)]) for g in range(GAUSS)]
    width = [by_type([-0.25 * cb_ref[g, t] for t in range(TYPES)]) for g in range(GAUSS)]
    level = by_type([cc_ref[t] for t in range(TYPES)])
    pad = jnp.zeros((LANES - TYPES, LANES), jnp.float32)

    def forms(b, where):
        s2 = jnp.zeros((TYPES, LANES), jnp.float32)
        for d in range(3):
            m = (jnp.broadcast_to(rows[b, d : d + 1, :], (TYPES, LANES)) - top).astype(jnp.float32)
            s2 = s2 + m * m
        s2 = s2 / (cell_edge * cell_edge)
        form = size[0] * jnp.exp(width[0] * s2)
        for g in range(1, GAUSS):
            form = form + size[g] * jnp.exp(width[g] * s2)
        form_rows[where, :] = jnp.concatenate([form + level, pad], axis=0).T

    forms(me_r, own_rows)
    folds[...] = jnp.zeros_like(folds)
    for copy in own_idx:
        copy.wait()
    kind = [type_ref[v * 8 : (v + 1) * 8, :] for v in range(tiles // 8)]

    ones = jnp.ones((8, LANES), jnp.bfloat16)

    def fold():
        for j in range(2):
            for g in range(half // 4):
                at = j * half * 8 + g * 32
                q = [folds[pl.ds(at + n, 8, stride=4), :] for n in range(4)]
                pairs[(j * half + g * 4) * 2 : (j * half + g * 4) * 2 + 8, :] = (q[0] + q[1]) + (q[2] + q[3])
        wide = [pairs[pl.ds(g * 16, 8, stride=2), :] + pairs[pl.ds(g * 16 + 1, 8, stride=2), :] for g in range(LANES // 8)]
        wide = jnp.concatenate(wide, axis=0)
        high = wide.astype(jnp.bfloat16)
        rest = (wide - high.astype(jnp.float32)).astype(jnp.bfloat16)
        lanes = (((1,), (1,)), ((), ()))
        total = lax.dot_general(ones, high, lanes, preferred_element_type=jnp.float32) + lax.dot_general(
            ones, rest, lanes, preferred_element_type=jnp.float32
        )
        return total[0:1, :]

    steps = 2 * n_refl
    per = 8
    chunks = steps // per
    hand_on = steps - 6

    def to_column(src, q, peer):
        return pltpu.make_async_remote_copy(
            src_ref=src, dst_ref=src, send_sem=c_send.at[q], recv_sem=c_recv.at[q],
            device_id=peer, device_id_type=MESH,
        )

    def to_plane(src, q, peer):
        return pltpu.make_async_remote_copy(
            src_ref=src, dst_ref=src, send_sem=p_send.at[q], recv_sem=p_recv.at[q],
            device_id=peer, device_id_type=MESH,
        )

    def rest_column(q):
        return to_column(in_column.at[q, pl.ds(0, len(turns))], q, column_peers[0])

    def rest_plane(q):
        return to_plane(in_plane.at[q, pl.ds(0, len(turns))], q, plane_peers[0])

    def send_column(q):
        for peer in column_peers:
            to_column(in_column.at[q, column], q, peer).start()

    def send_plane(q):
        rest_column(q).wait_recv()
        in_plane[q, plane] = jnp.sum(in_column[q], axis=0)
        for peer in plane_peers:
            to_plane(in_plane.at[q, plane], q, peer).start()

    def step_at(i):
        later = i - 2
        return jnp.where(i < 2, 2 * me_r + i, jnp.where(later < 2 * me_r, later, i))

    def picks_copies():
        return [pltpu.make_async_copy(idx_v.at[d, 0], picks[d], i_sem.at[d]) for d in range(3)]

    def prepare():
        all_of(rows, g_send, g_recv, n_refl - 1).wait_recv()
        for b in range(n_refl):
            for d in range(3):
                idx_v[d, :, b * LANES : (b + 1) * LANES] = rows[b, d : d + 1, :]
        for copy in picks_copies():
            copy.start()
        for b in range(n_refl):
            forms(b, pl.ds(b * LANES, LANES))

    def forward_step(i, _):
        @pl.when(i == 2)
        def _():
            prepare()
            for copy in picks_copies():
                copy.wait()

        @pl.when(i == hand_on)
        def _():
            send_plane(0)

        n = step_at(i)
        before = step_at(lax.rem(i + steps - 1, steps))
        in_column[lax.div(before, per), column, pl.ds(lax.rem(before, per), 1), :] = fold()
        r0 = n * half
        for u in range(half):
            r = r0 + u
            h, k, l = hs[r], ks[r], ls[r]
            form_row = jnp.broadcast_to(form_rows[pl.ds(r, 1), :], (8, LANES))
            real, imag = None, None
            for v in range(tiles // 8):
                off = v * 8
                c, s = rotate(
                    tx[h, 0, off : off + 8, :], tx[h, 1, off : off + 8, :],
                    ty[k, 0, off : off + 8, :], ty[k, 1, off : off + 8, :],
                )
                c, s = rotate(c, s, tz[l, 0, off : off + 8, :], tz[l, 1, off : off + 8, :])
                form = jnp.take_along_axis(form_row, kind[v], axis=1, mode="promise_in_bounds")
                c = c * form
                s = s * form
                store[r, 0, off : off + 8, :] = c
                store[r, 1, off : off + 8, :] = s
                real = c if real is None else real + c
                imag = s if imag is None else imag + s
            folds[u * 8 : u * 8 + 8, :] = real
            folds[(half + u) * 8 : (half + u) * 8 + 8, :] = imag

        @pl.when(jnp.logical_and(i > 2, lax.div(n, per) > lax.div(before, per)))
        def _():
            send_column(lax.div(before, per))

        return 0

    lax.fori_loop(0, steps, forward_step, 0)
    last = step_at(steps - 1)
    in_column[chunks - 1, column, pl.ds(lax.rem(last, per), 1), :] = fold()
    send_column(chunks - 1)

    atoms = tiles * LANES * n_atom * n_refl
    inv_atoms = 1.0 / math.sqrt(atoms)
    factor = 2.0 / math.sqrt(refl)
    low = lax.broadcasted_iota(jnp.int32, (per, LANES), 1) < half

    def spread(row):
        return jnp.broadcast_to(row, (LANES, LANES)).T

    all_of(ow, o_send, o_recv, n_refl - 1).wait_recv()
    low_row = lax.broadcasted_iota(jnp.int32, (1, LANES), 1) < half
    for b in range(n_refl):
        for q in range(2):
            row = ow[b, q : q + 1, :]
            turned = pltpu.roll(row, half, 1)
            seen[q, 2 * b : 2 * b + 1, :] = jnp.where(low_row, row, turned)
            seen[q, 2 * b + 1 : 2 * b + 2, :] = jnp.where(low_row, turned, row)

    send_plane(1)
    for b in range(n_refl):
        for d, wide in enumerate((wide_h, wide_k, wide_l)):
            wide[b * LANES : (b + 1) * LANES, :] = spread((rows[b, d : d + 1, :] - top).astype(jnp.float32))
    send_plane(2)

    def totals(q):
        rest_plane(q).wait_recv()
        both = jnp.sum(in_plane[q], axis=0) * inv_atoms
        square = both * both
        amp = jnp.sqrt(square + pltpu.roll(square, half, 1) + 0.25)
        return both, amp, seen[0, q * per : (q + 1) * per, :], seen[1, q * per : (q + 1) * per, :]

    def place(q, values, first, second):
        for i in range(per):
            at = (q * per + i) * half
            block = spread(values[i : i + 1, :])
            first[at : at + half, :] = block[:half]
            second[at : at + half, :] = block[half:]

    def both_sums(q, both, amp, obs, weight):
        place(q, both, wide_a, wide_b)
        place(q, jnp.where(low, factor * weight, factor * weight * obs / amp), wide_1, wide_2)

    def wide_rows(r, sources):
        return [jnp.broadcast_to(w[pl.ds(r, 1), :], (8, LANES)) for w in sources]

    def early(i, acc):
        acc = [[list(a) for a in g] for g in acc]
        r0 = i * unroll_b
        for u in range(unroll_b):
            r = r0 + u
            a, b, w1, w2, *m = wide_rows(r, (wide_a, wide_b, wide_1, wide_2, wide_h, wide_k, wide_l))
            for v in range(tiles // 8):
                off = v * 8
                p = b * store[r, 0, off : off + 8, :] - a * store[r, 1, off : off + 8, :]
                for g, w in enumerate((w1, w2)):
                    inner = w * p
                    for d in range(3):
                        acc[g][d][v] = acc[g][d][v] + m[d] * inner
        return tuple(tuple(tuple(a) for a in g) for g in acc)

    def late(i, acc):
        acc = [list(a) for a in acc]
        r0 = i * unroll_b
        for u in range(unroll_b):
            r = r0 + u
            a, b, *m = wide_rows(r, (wide_a, wide_b, wide_h, wide_k, wide_l))
            for v in range(tiles // 8):
                off = v * 8
                inner = b * store[r, 0, off : off + 8, :] - a * store[r, 1, off : off + 8, :]
                for d in range(3):
                    acc[d][v] = acc[d][v] + m[d] * inner
        return tuple(tuple(a) for a in acc)

    none = jnp.zeros((8, LANES), jnp.float32)
    group = ((none,) * (tiles // 8),) * 3
    size_q = per * half // unroll_b
    known = []
    acc2 = (group, group)
    for q in range(chunks - 1):
        known.append(totals(q))
        both_sums(q, *known[q])
        middle = q * size_q + size_q // 2
        acc2 = lax.fori_loop(q * size_q, middle, early, acc2)
        if q == 1:
            send_plane(chunks - 1)
        acc2 = lax.fori_loop(middle, (q + 1) * size_q, early, acc2)
    known.append(totals(chunks - 1))

    over = sum(jnp.where(low, weight * obs * amp, 0.0) for _, amp, obs, weight in known)
    under = sum(jnp.where(low, weight * amp * amp, 0.0) for _, amp, obs, weight in known)
    over = jnp.sum(over, axis=(0, 1), keepdims=True)
    under = jnp.sum(under, axis=(0, 1), keepdims=True)
    scale = over / under
    for q, (both, amp, obs, weight) in enumerate(known):
        seen[0, q * per : (q + 1) * per, :] = scale * amp
        if q == chunks - 1:
            place(q, factor * weight * scale * (scale * amp - obs) / amp * both, wide_a, wide_b)
    acc = lax.fori_loop((chunks - 1) * size_q, chunks * size_q, late, group)
    for d in range(3):
        for v in range(tiles // 8):
            total = acc[d][v] + scale * (scale * acc2[0][d][v] - acc2[1][d][v])
            for a in range(8):
                t = v * 8 + a
                grad_ref[d : d + 1, t * LANES : (t + 1) * LANES] = total[a : a + 1, :]
    resid_ref[...] = jnp.where(low_row, seen[0, pl.ds(2 * me_r, 1), :], seen[0, pl.ds(2 * me_r + 1, 1), :])

    all_of(rows, g_send, g_recv, n_refl - 1).wait_send()
    all_of(ow, o_send, o_recv, n_refl - 1).wait_send()
    for q in range(chunks):
        rest_column(q).wait_send()
        rest_plane(q).wait_send()


def solution(mesh):
    n_atom, n_refl = mesh.shape["atom"], mesh.shape["refl"]

    def local(positions, occupancy, bfactor, atom_type, miller, observed, weight, coef_a, coef_b, coef_c):
        shard = positions.shape[1]
        tiles = shard // LANES
        refl = miller.shape[1] * n_refl
        vmem = pl.BlockSpec(memory_space=pltpu.VMEM)
        f32 = jnp.float32
        table = pltpu.VMEM((2 * top + 1, 2, tiles, LANES), f32)
        wide = pltpu.VMEM((refl, LANES), f32)
        smem_row = pltpu.SMEM((refl,), jnp.int32)
        dma = pltpu.SemaphoreType.DMA
        chunks = 2 * n_refl // 8
        gradient, residual = pl.pallas_call(
            functools.partial(kernel, n_atom, n_refl),
            out_shape=(
                pltpu.VMEM((3, shard), f32),
                pltpu.VMEM((1, LANES), f32),
            ),
            in_specs=[pl.BlockSpec(memory_space=pl.ANY)] * 10,
            out_specs=(vmem, vmem),
            scratch_shapes=[
                pltpu.VMEM((3, shard), f32),
                pltpu.VMEM((tiles, LANES), f32),
                pltpu.VMEM((tiles, LANES), f32),
                pltpu.VMEM((tiles, LANES), jnp.int32),
                pltpu.VMEM((3, LANES), jnp.int32),
                pltpu.VMEM((1, LANES), f32),
                pltpu.VMEM((1, LANES), f32),
                pltpu.SMEM((GAUSS, TYPES), f32),
                pltpu.SMEM((GAUSS, TYPES), f32),
                pltpu.SMEM((TYPES,), f32),
                table, table, table,
                pltpu.VMEM((refl, 2, tiles, LANES), f32),
                wide,
                pltpu.VMEM((n_refl, 3, LANES), jnp.int32),
                pltpu.VMEM((3, 1, refl), jnp.int32),
                smem_row, smem_row, smem_row,
                pltpu.VMEM((8 * LANES, LANES), f32),
                pltpu.VMEM((2 * LANES, LANES), f32),
                pltpu.VMEM((2, 2 * n_refl, LANES), f32),
                pltpu.VMEM((n_refl, 2, LANES), f32),
                pltpu.VMEM((chunks, SIDE * SIDE, 8, LANES), f32),
                pltpu.VMEM((chunks, SIDE * SIDE, 8, LANES), f32),
                wide, wide, wide, wide, wide, wide, wide,
                dma, dma, dma, dma,
                dma((chunks,)), dma((chunks,)), dma((chunks,)), dma((chunks,)),
                dma((3,)), dma((3,)), dma((10,)),
            ],
            compiler_params=pltpu.CompilerParams(
                collective_id=0, has_side_effects=True, vmem_limit_bytes=58 * 2**20
            ),
        )(
            positions,
            occupancy.reshape(tiles, LANES),
            bfactor.reshape(tiles, LANES),
            atom_type.reshape(tiles, LANES),
            miller,
            observed.reshape(1, LANES),
            weight.reshape(1, LANES),
            coef_a.T, coef_b.T, coef_c,
        )
        inv_atoms = 1.0 / math.sqrt(shard * n_atom * n_refl)
        return gradient * (two_pi * inv_atoms), residual.reshape(LANES) - observed

    split = P(("atom", "refl"))
    return jax.shard_map(
        local,
        mesh=mesh,
        in_specs=(
            P(None, ("atom", "refl")), split, split, split,
            P(None, "refl"), P("refl"), P("refl"), P(), P(), P(),
        ),
        out_specs=(P(None, ("atom", "refl")), P("refl")),
        check_vma=False,
    )
```
